128 devices in a mesh: gx: 16 (over z, y), yz: 8 (over x, core).
Axes of the slice: x: 4, y: 4, z: 4, core: 2. Of those that a mesh axis runs over, the one named last changes fastest.
Arguments:
- positions: float32 [3, 8192, 256], P(None, ('gx', 'yz')), may hold values from -3 to 3
- velocity: float32 [3, 8192, 256], P(None, ('gx', 'yz')), may hold values from -6 to 6
- energy: float32 [8192, 256], P(('gx', 'yz')), may hold values from 0.5 to 2
- masses: float32 [8192, 256], P(('gx', 'yz')), may hold values from 0.002 to 0.008
- smoothing_bins: int32 [8192, 256], P(('gx', 'yz')), may hold values from 0 to 5
- counts: int32 [8192], P(('gx', 'yz')), may hold values from 8 to 256, as said below
- exports: int32 [4096], P(('gx', 'yz')), may hold values from 0 to 63, as said below
- cross_pairs: int32 [2, 32768], P(None, ('gx', 'yz')), may hold values from 0 to 287, as said below
- local_pairs: int32 [2, 8192], P(None, ('gx', 'yz')), may hold values from 0 to 63, as said below
Outputs:
- density: float32 [8192, 256], P(('gx', 'yz'))
- acceleration: float32 [3, 8192, 256], P(None, ('gx', 'yz'))
- energy_rate: float32 [8192, 256], P(('gx', 'yz'))
The draws below stay inside these ranges and needn't reach their ends.
Inputs may be any that keep to these rules, and one draw needn't show every extreme that they name: `counts`: each device has some cell holding exactly 256 live particles; the mean count differs from device to device. `exports`: each device's block of 32 entries lists distinct local cells. `cross_pairs`: row 0 is a local cell of the device that holds the column; row 1 is an import slot (3 a + b) * 32 + k with (a, b) never (1, 1). A device's block of 256 columns holds 32 columns for each of the directions (a, b) = (1, 2), (2, 0), (2, 1), (2, 2), then for (1, 0), (0, 2), (0, 1), (0, 0). Each column of the first half is mirrored by exactly one column of the second half on the device that owns its imported cell, naming the same two cells, and no two columns of a block name the same two cells. `local_pairs`: both rows hold local cells of the device that holds the column; they differ in every column.
All inputs are finite; a program needn't handle non-finite values.
Results may differ from the reference program's by a relative error of at most 0.0003.
Values sent between devices are 32-bit elements; how exact they have to be, the bound alone decides.
A program may use at most 64 MiB of HBM per device.

```python
import math
import jax
import jax.numpy as jnp
from jax import lax

CELL_SLOTS = 256
CELLS_DEV = 64
EXPORT = 32
LOCAL_PAIRS = 64
CROSS_PAIRS = 256
CELLS = 8192
N_GX = 16
N_YZ = 8
DEVICES = 128


def pick_export(single_key):
    return jax.random.permutation(single_key, CELLS_DEV)[:EXPORT]


def pick_order(single_key):
    return jax.random.permutation(single_key, EXPORT)


def export_table(key):
    keys = jax.random.split(jax.random.fold_in(key, 101), DEVICES)
    return jax.vmap(pick_export)(keys).astype(jnp.int32)


def draw_exports(key, part):
    return export_table(key).reshape(DEVICES * EXPORT)


def draw_cross_pairs(key, part):
    table = export_table(key)
    key = jax.random.fold_in(key, 7)
    link_keys = jax.random.split(key, DEVICES * 4)
    orders = jax.vmap(pick_order)(link_keys).astype(jnp.int32).reshape(DEVICES, 4, EXPORT)
    device_ids = jnp.arange(DEVICES, dtype=jnp.int32)
    row_ids = device_ids // N_YZ
    col_ids = device_ids % N_YZ
    within = jnp.broadcast_to(jnp.arange(EXPORT, dtype=jnp.int32)[None, :], (DEVICES, EXPORT))
    cell_lists = []
    slot_lists = []
    for turn in range(4):
        cell_lists.append(table)
        slot_lists.append((5 + turn) * EXPORT + orders[:, turn, :])
    for turn in range(4):
        mirror = 3 - turn
        partner = (row_ids + mirror // 3 - 1) % N_GX * N_YZ + (col_ids + mirror % 3 - 1) % N_YZ
        cell_lists.append(jnp.take_along_axis(table, orders[partner, turn, :], axis=1))
        slot_lists.append(mirror * EXPORT + within)
    cell_part = jnp.stack(cell_lists, axis=1).reshape(-1)
    slot_part = jnp.stack(slot_lists, axis=1).reshape(-1)
    return jnp.stack([cell_part, slot_part], axis=0).astype(jnp.int32)


def draw_counts(key, part):
    key = jax.random.fold_in(key, 3)
    first, second, third = jax.random.split(key, 3)
    ceiling = jax.random.randint(first, (DEVICES, 1), CELL_SLOTS // 4, CELL_SLOTS + 1)
    spread = jax.random.randint(second, (DEVICES, CELLS_DEV), 0, CELL_SLOTS)
    filled = 8 + spread % (ceiling - 7)
    full_cell = jax.random.randint(third, (DEVICES, 1), 0, CELLS_DEV)
    cell_ids = jnp.arange(CELLS_DEV, dtype=jnp.int32)[None, :]
    return jnp.where(cell_ids == full_cell, CELL_SLOTS, filled).reshape(CELLS).astype(jnp.int32)


def draw_local_pairs(key, part):
    key = jax.random.fold_in(key, 5)
    first, second = jax.random.split(key, 2)
    target = jax.random.randint(first, (DEVICES * LOCAL_PAIRS,), 0, CELLS_DEV)
    stride = jax.random.randint(second, (DEVICES * LOCAL_PAIRS,), 1, CELLS_DEV)
    source = (target + stride) % CELLS_DEV
    return jnp.stack([target, source], axis=0).astype(jnp.int32)


def touch_ends(array, key, smallest, high):
    index_at = [jax.random.randint(jax.random.fold_in(key, axis), (), 0, length) for axis, length in enumerate(array.shape)]
    main_axis = array.shape.index(max(array.shape))
    beside = index_at[:main_axis] + [(index_at[main_axis] + 1) % array.shape[main_axis]] + index_at[main_axis + 1:]
    return array.at[tuple(index_at)].set(smallest).at[tuple(beside)].set(high)


def level_of(rng, extent, shards, least, top_value):
    gain, own = 1.0, jax.random.fold_in(rng, 6)
    for position, parts in shards:
        draws = jnp.exp(jax.random.uniform(jax.random.fold_in(own, position), (parts,), jnp.float32, least / len(shards), top_value / len(shards)))
        gain = gain * jnp.repeat(draws, extent[position] // parts).reshape([-1 if axis == position else 1 for axis in range(len(extent))])
    return gain


def noise(rng, shape, scale, reach, cuts=(), held_as=jnp.bfloat16):
    values = scale * jax.random.normal(rng, shape, jnp.float32)
    if cuts:
        values = values * level_of(rng, shape, cuts, -0.22, 0.18)
    return jnp.clip(values, -reach, reach).astype(held_as)


def setup_inputs(seed: int = 0) -> dict:
    key_list = jax.random.split(jax.random.key(seed), 10)
    positions = noise(key_list[0], (3, CELLS, CELL_SLOTS), 0.5, 3.0, ((1, 128),), jnp.float32)
    velocity = noise(key_list[1], (3, CELLS, CELL_SLOTS), 1.0, 6.0, ((1, 128),), jnp.float32)
    energy = jnp.clip(jnp.exp(math.log(2.0) - 1.3862944 * jax.random.uniform(key_list[2], (CELLS, CELL_SLOTS), jnp.float32) ** level_of(key_list[2], (CELLS, CELL_SLOTS), ((0, 128),), -0.2, 0.2)), 0.5, 2.0)
    masses = jnp.clip(jnp.exp(math.log(0.008) - 1.3862944 * jax.random.uniform(key_list[3], (CELLS, CELL_SLOTS), jnp.float32) ** level_of(key_list[3], (CELLS, CELL_SLOTS), ((0, 128),), -0.2, 0.2)), 0.002, 0.008)
    smoothing_bins = touch_ends(jax.random.randint(key_list[4], (CELLS, CELL_SLOTS), 0, 6), jax.random.fold_in(key_list[4], 1), 0, 5).astype(jnp.int32)
    counts = draw_counts(jax.random.fold_in(key_list[9], 71), 0)
    exports = draw_exports(jax.random.fold_in(key_list[9], 71), 0)
    cross_pairs = draw_cross_pairs(jax.random.fold_in(key_list[9], 71), 0)
    local_pairs = draw_local_pairs(jax.random.fold_in(key_list[9], 71), 0)
    return dict(positions=positions, velocity=velocity, energy=energy, masses=masses, smoothing_bins=smoothing_bins, counts=counts, exports=exports, cross_pairs=cross_pairs, local_pairs=local_pairs)


SIGMA_NORM = 0.3183098861837907
GAMMA_GAS = 5.0 / 3.0
ALPHA_VISC = 1.0
BETA_VISC = 2.0

def spline_value(scaled):
    inner_part = 1.0 - 1.5 * scaled ** 2 + 0.75 * scaled ** 3
    outer_part = 0.25 * jnp.maximum(2.0 - scaled, 0.0) ** 3
    return jnp.where(scaled < 1.0, inner_part, outer_part)

def spline_slope(scaled):
    inner_part = -3.0 + 2.25 * scaled
    outer_part = -0.75 * jnp.maximum(2.0 - scaled, 0.0) ** 2 / jnp.maximum(scaled, 1.0)
    return jnp.where(scaled < 1.0, inner_part, outer_part)

def separation(target, source):
    diff_x = target[:, 0, :, None] - source[:, 0, None, :]
    diff_y = target[:, 1, :, None] - source[:, 1, None, :]
    diff_z = target[:, 2, :, None] - source[:, 2, None, :]
    return (diff_x, diff_y, diff_z)

def density_block(target, source):
    diff_x, diff_y, diff_z = separation(target, source)
    radius = jnp.sqrt(diff_x * diff_x + diff_y * diff_y + diff_z * diff_z)
    smooth = target[:, 3, :, None]
    weight = spline_value(radius / smooth) * (SIGMA_NORM / smooth ** 3)
    return lax.optimization_barrier(jnp.sum(weight * source[:, 4, None, :], axis=2))

def force_block(target, source):
    diff_x, diff_y, diff_z = separation(target, source)
    dist_sq = diff_x * diff_x + diff_y * diff_y + diff_z * diff_z
    radius = jnp.sqrt(dist_sq)
    smooth_target = target[:, 3, :, None]
    smooth_source = source[:, 3, None, :]
    grad_mean = 0.5 * (spline_slope(radius / smooth_target) * (SIGMA_NORM / smooth_target ** 5) + spline_slope(radius / smooth_source) * (SIGMA_NORM / smooth_source ** 5))
    vel_x = target[:, 5, :, None] - source[:, 5, None, :]
    vel_y = target[:, 6, :, None] - source[:, 6, None, :]
    vel_z = target[:, 7, :, None] - source[:, 7, None, :]
    approach = vel_x * diff_x + vel_y * diff_y + vel_z * diff_z
    smooth_mean = 0.5 * (smooth_target + smooth_source)
    converge = smooth_mean * jnp.minimum(approach, 0.0) / (dist_sq + 0.01 * smooth_mean ** 2)
    sound_mean = 0.5 * (target[:, 10, :, None] + source[:, 10, None, :])
    density_mean = 0.5 * (target[:, 8, :, None] + source[:, 8, None, :])
    viscous = (BETA_VISC * converge ** 2 - ALPHA_VISC * sound_mean * converge) / density_mean
    press_target = target[:, 9, :, None]
    press_source = source[:, 9, None, :]
    common = (press_target + press_source + viscous) * grad_mean
    mass_target = target[:, 4, :, None]
    mass_source = source[:, 4, None, :]
    pull_target = mass_source * common
    pull_source = mass_target * common
    work_rate = grad_mean * approach
    target_part = jnp.stack([-lax.optimization_barrier(jnp.sum(pull_target * diff_x, axis=2)), -lax.optimization_barrier(jnp.sum(pull_target * diff_y, axis=2)), -lax.optimization_barrier(jnp.sum(pull_target * diff_z, axis=2)), lax.optimization_barrier(jnp.sum(mass_source * (press_target + 0.5 * viscous) * work_rate, axis=2))], axis=1)
    source_part = jnp.stack([lax.optimization_barrier(jnp.sum(pull_source * diff_x, axis=1)), lax.optimization_barrier(jnp.sum(pull_source * diff_y, axis=1)), lax.optimization_barrier(jnp.sum(pull_source * diff_z, axis=1)), lax.optimization_barrier(jnp.sum(mass_target * (press_source + 0.5 * viscous) * work_rate, axis=1))], axis=1)
    return (target_part, source_part)

def density_pass(cell_data, source_table, targets, sources):
    cell_count = cell_data.shape[0]
    slot_count = cell_data.shape[2]
    block_count = targets.shape[0] // 16
    cell_range = jnp.arange(cell_count, dtype=jnp.int32)

    def accumulate(running, id_pair):
        target_ids, source_ids = id_pair
        contribution = density_block(cell_data[target_ids], source_table[source_ids])
        select = (cell_range[:, None] == target_ids[None, :]).astype(jnp.float32)
        added = jnp.dot(select, contribution, precision=lax.Precision.HIGHEST, preferred_element_type=jnp.float32)
        return (running + added, None)
    running, unused = lax.scan(accumulate, jnp.zeros((cell_count, slot_count), jnp.float32), (targets.reshape(block_count, 16), sources.reshape(block_count, 16)))
    return running

def force_pass(cell_data, source_table, targets, sources, return_slots, slot_total):
    cell_count = cell_data.shape[0]
    slot_count = cell_data.shape[2]
    block_count = targets.shape[0] // 16
    cell_range = jnp.arange(cell_count, dtype=jnp.int32)
    slot_range = jnp.arange(slot_total, dtype=jnp.int32)

    def accumulate(carried, id_triple):
        own_sum, returned = carried
        target_ids, source_ids, slot_ids = id_triple
        target_part, source_part = force_block(cell_data[target_ids], source_table[source_ids])
        select = (cell_range[:, None] == target_ids[None, :]).astype(jnp.float32)
        select_slot = (slot_range[:, None] == slot_ids[None, :]).astype(jnp.float32)
        own_sum = own_sum + jnp.dot(select, target_part.reshape(16, 4 * slot_count), precision=lax.Precision.HIGHEST, preferred_element_type=jnp.float32)
        returned = returned + jnp.dot(select_slot, source_part.reshape(16, 4 * slot_count), precision=lax.Precision.HIGHEST, preferred_element_type=jnp.float32)
        return ((own_sum, returned), None)
    start = (jnp.zeros((cell_count, 4 * slot_count), jnp.float32), jnp.zeros((slot_total, 4 * slot_count), jnp.float32))
    carried, unused = lax.scan(accumulate, start, (targets.reshape(block_count, 16), sources.reshape(block_count, 16), return_slots.reshape(block_count, 16)))
    return carried

def neighbour_cells(exports):
    device_ids = jnp.arange(DEVICES, dtype=jnp.int32)
    row_ids = device_ids // N_YZ
    col_ids = device_ids % N_YZ
    export_grid = exports.reshape(DEVICES, EXPORT)
    listing = []
    for direction in range(9):
        partner = (row_ids + direction // 3 - 1) % N_GX * N_YZ + (col_ids + direction % 3 - 1) % N_YZ
        listing.append(partner[:, None] * CELLS_DEV + export_grid[partner])
    return jnp.stack(listing, axis=1).reshape(DEVICES, 9 * EXPORT).astype(jnp.int32)

def reference(positions, velocity, energy, masses, smoothing_bins, counts, exports, cross_pairs, local_pairs):
    live_mask = (lax.broadcasted_iota(jnp.int32, (CELLS, CELL_SLOTS), 1) < counts[:, None]).astype(jnp.float32)
    smooth = 0.4 * 1.2 ** smoothing_bins.astype(jnp.float32)
    particle_mass = masses * live_mask
    base = jnp.concatenate([jnp.transpose(positions, (1, 0, 2)), smooth[:, None], particle_mass[:, None]], axis=1)
    import_ids = neighbour_cells(exports)
    cross_grid = cross_pairs.reshape(2, DEVICES, CROSS_PAIRS)
    local_grid = local_pairs.reshape(2, DEVICES, LOCAL_PAIRS)
    cell_range = jnp.arange(CELLS_DEV, dtype=jnp.int32)
    device_list = jnp.arange(DEVICES, dtype=jnp.int32)

    def density_device(device_id):
        cell_data = lax.dynamic_slice_in_dim(base, device_id * CELLS_DEV, CELLS_DEV, 0)
        source_table = jnp.concatenate([cell_data, base[import_ids[device_id]]], axis=0)
        targets = jnp.concatenate([cell_range, local_grid[0, device_id], cross_grid[0, device_id]])
        sources = jnp.concatenate([cell_range, local_grid[1, device_id], cross_grid[1, device_id] + CELLS_DEV])
        return density_pass(cell_data, source_table, targets, sources)
    raw_density = lax.map(density_device, device_list).reshape(CELLS, CELL_SLOTS)
    rho = jnp.where(live_mask > 0, raw_density, 1.0)
    pressure_term = (GAMMA_GAS - 1.0) * energy / rho
    sound_speed = jnp.sqrt(GAMMA_GAS * (GAMMA_GAS - 1.0) * energy)
    new_fields = jnp.stack([velocity[0], velocity[1], velocity[2], rho, pressure_term, sound_speed], axis=1)
    forcing = jnp.concatenate([base, new_fields], axis=1)
    upper_count = CROSS_PAIRS // 2

    def force_device(device_id):
        cell_data = lax.dynamic_slice_in_dim(forcing, device_id * CELLS_DEV, CELLS_DEV, 0)
        source_table = jnp.concatenate([cell_data, forcing[import_ids[device_id]]], axis=0)
        upper_pairs = cross_grid[:, device_id, :upper_count]
        targets = jnp.concatenate([cell_range, local_grid[0, device_id], upper_pairs[0]])
        sources = jnp.concatenate([cell_range, local_grid[1, device_id], upper_pairs[1] + CELLS_DEV])
        return_slots = jnp.concatenate([-jnp.ones((CELLS_DEV + LOCAL_PAIRS,), jnp.int32), upper_pairs[1]])
        return force_pass(cell_data, source_table, targets, sources, return_slots, 9 * EXPORT)
    own_sums, returns = lax.map(force_device, device_list)
    totals = own_sums.reshape(CELLS, 4 * CELL_SLOTS)
    totals = totals.at[import_ids.reshape(-1)].add(returns.reshape(DEVICES * 9 * EXPORT, 4 * CELL_SLOTS))
    totals = totals.reshape(CELLS, 4, CELL_SLOTS)
    acceleration = jnp.transpose(totals[:, :3], (1, 0, 2)) * live_mask[None]
    energy_rate = totals[:, 3] * live_mask
    return (raw_density * live_mask, acceleration, energy_rate)
```

```python
import functools
import math

import jax
import jax.numpy as jnp
from jax import lax
from jax.experimental import pallas as pl
from jax.experimental.pallas import tpu as pltpu
from jax.sharding import PartitionSpec as P

F32 = jnp.float32
SIGMA_NORM = 0.3183098861837907
GAMMA_GAS = 5.0 / 3.0
TINY = 1e-24
CELLS, SLOTS, EXPORT = 64, 256, 32
DENSITY_ROWS = 64
FORCE_ROWS = 32
VMEM, SMEM = pltpu.VMEM, pltpu.SMEM
HALF_BETA, BETA_H, SOUND, RHO, PRESS, TENTH_H = range(6)


def lanes_of(wide):
    return (0, 128) if wide else (0,)


def by_width(flag, block):
    @pl.when(flag)
    def wide_block():
        block((0, 128))

    @pl.when(jnp.logical_not(flag))
    def narrow_block():
        block((0,))


def spread(rows, target, count):
    def half(start):
        for slot, row in rows:
            part = row(start)
            target[slot, pl.ds(start, 128), :] = jnp.transpose(jnp.broadcast_to(part, (128, 128)))

    half(0)

    @pl.when(count > 128)
    def second_half():
        half(128)


def cell_row(table, cell, row):
    return lambda start: table[cell, row : row + 1, start : start + 128]


def summed_rows(values):
    return jnp.sum(values.reshape(values.shape[0] // 8, 8, 128), axis=0)


def spline_unscaled(dist_sq, smooth_twice, smooth):
    dist_sq = jnp.maximum(dist_sq, TINY)
    radius = dist_sq * lax.rsqrt(dist_sq)
    outer = jnp.maximum(smooth_twice - radius, 0.0)
    inner = jnp.maximum(smooth - radius, 0.0)
    return (0.25 * outer) * (outer * outer) - inner * (inner * inner)


def prepare_kernel(counts, exports, pos, vel, energy, masses, bins, table, near, far):
    lane = lax.broadcasted_iota(jnp.int32, (1, SLOTS), 1)
    for cell in range(CELLS):
        live = (lane < counts[cell]).astype(F32)
        one = slice(cell, cell + 1)
        for axis in range(3):
            table[cell, axis : axis + 1, :] = pos[axis, one, :]
            table[cell, 5 + axis : 6 + axis, :] = vel[axis, one, :]
        table[cell, 3:4, :] = masses[one, :] * live
        table[cell, 4:5, :] = 0.4 * jnp.exp2(bins[one, :].astype(F32) * math.log2(1.2))
        table[cell, 8:9, :] = energy[one, :]
        table[cell, 9:10, :] = live

    def gather(k, carry):
        near[k] = table[exports[k], 0:4, :]
        far[k] = table[exports[k], 4:8, :]
        return carry

    lax.fori_loop(0, EXPORT, gather, 0)


def density_local_kernel(counts, starts, listed, table, raw, held):
    raw[...] = jnp.zeros_like(raw)
    size = DENSITY_ROWS

    def per_cell(cell, carry):
        count = counts[cell]
        spread([(i, cell_row(table, cell, i)) for i in range(4)], held, count)
        trips = (count + (size - 1)) // size

        def pair(target):
            def block(lanes):
                fields = []
                for l in lanes:
                    x, y, z, h = (table[target, i : i + 1, l : l + 128] for i in (0, 1, 2, 4))
                    fields.append((x, y, z, h + h, h))

                def chunk(step, totals):
                    rows = pl.ds(pl.multiple_of(step * size, size), size)
                    sx, sy, sz, mass = (held[i, rows, :] for i in range(4))
                    result = []
                    for total, (x, y, z, h2, h1) in zip(totals, fields):
                        dx, dy, dz = x - sx, y - sy, z - sz
                        weight = spline_unscaled(dx * dx + dy * dy + dz * dz, h2, h1)
                        result.append(total + summed_rows(weight * mass))
                    return tuple(result)

                totals = lax.fori_loop(0, trips, chunk, (jnp.zeros((8, 128), F32),) * len(lanes))
                for l, total in zip(lanes, totals):
                    raw[target, :, l : l + 128] += jnp.sum(total, axis=0, keepdims=True)

            by_width(counts[target] > 128, block)

        pair(cell)
        lax.fori_loop(starts[cell], starts[cell + 1], lambda j, c: (pair(listed[j]), c)[1], 0)
        return carry

    lax.fori_loop(0, CELLS, per_cell, 0)


def density_cross_kernel(
    counts, exports, starts, listed, wide, table, partial, i0, i1, i2, i3, i5, i6, i7, i8, raw, late,
    imports, held, sums,
):
    size = DENSITY_ROWS
    for direction, block in enumerate((i0, i1, i2, i3, None, i5, i6, i7, i8)):
        if block is not None:
            imports[direction * EXPORT : (direction + 1) * EXPORT] = block[...]

    def per_cell(cell, carry):
        count = counts[cell]
        raw[cell] = partial[cell]

        @pl.when(starts[cell + 1] > starts[cell])
        def with_pairs():
            spread([(i, cell_row(table, cell, r)) for i, r in enumerate((0, 1, 2, 4))], held, count)
            trips = (count + (size - 1)) // size
            sums[...] = jnp.zeros_like(sums)

            def pair(source):
                def block(lanes):
                    fields = [
                        tuple(imports[source, i : i + 1, l : l + 128] for i in range(4)) for l in lanes
                    ]

                    def chunk(step, carry):
                        rows = pl.ds(pl.multiple_of(step * size, size), size)
                        tx, ty, tz, h1 = (held[i, rows, :] for i in range(4))
                        h2 = h1 + h1
                        total = sums[rows, :]
                        for x, y, z, mass in fields:
                            dx, dy, dz = x - tx, y - ty, z - tz
                            weight = spline_unscaled(dx * dx + dy * dy + dz * dz, h2, h1)
                            total = total + weight * mass
                        sums[rows, :] = total
                        return carry

                    lax.fori_loop(0, trips, chunk, 0)

                by_width(wide[source] > 0, block)

            lax.fori_loop(starts[cell], starts[cell + 1], lambda j, c: (pair(listed[j]), c)[1], 0)
            for l in (0, 128):
                flipped = jnp.transpose(sums[l : l + 128, :])
                raw[cell, :, l : l + 128] += jnp.sum(flipped, axis=0, keepdims=True)

        inverse = pl.reciprocal(table[cell, 4:5, :], approx=False)
        cube = inverse * inverse * inverse
        raw[cell] = raw[cell] * (SIGMA_NORM * cube * cube)
        return carry

    lax.fori_loop(0, CELLS, per_cell, 0)

    def gather(k, carry):
        cell = exports[k]
        late[k, 0:1, :] = jnp.where(table[cell, 9:10, :] > 0, raw[cell], 1.0)
        late[k, 1:2, :] = table[cell, 8:9, :]
        return carry

    lax.fori_loop(0, EXPORT, gather, 0)


def force_fields(target, cell, smooth, rho, energy):
    root = math.sqrt(1.5 * SIGMA_NORM)
    inverse = pl.reciprocal(smooth, approx=False)
    square = inverse * inverse
    target[cell, HALF_BETA : HALF_BETA + 1, :] = (0.5 * root) * (square * inverse)
    target[cell, BETA_H : BETA_H + 1, :] = root * square
    target[cell, SOUND : SOUND + 1, :] = jnp.sqrt(GAMMA_GAS * (GAMMA_GAS - 1.0) * energy) * (1.0 / 40.0)
    target[cell, RHO : RHO + 1, :] = rho * (1.0 / 200.0)
    target[cell, PRESS : PRESS + 1, :] = (GAMMA_GAS - 1.0) * energy / rho
    target[cell, TENTH_H : TENTH_H + 1, :] = 0.05 * smooth


def local_force_fields(table, raw, extra):
    def one(cell, carry):
        rho = jnp.where(table[cell, 9:10, :] > 0, raw[cell], 1.0)
        force_fields(extra, cell, table[cell, 4:5, :], rho, table[cell, 8:9, :])
        return carry

    lax.fori_loop(0, CELLS, one, 0)


def slope_part(radius, half_beta, beta_h):
    reach = half_beta * radius
    outer = jnp.maximum(beta_h - reach, 0.0)
    least = jnp.minimum(outer, reach)
    return least * (outer + (outer - least))


def force_pair(row, lane):
    dx, dy, dz = lane[0] - row[0], lane[1] - row[1], lane[2] - row[2]
    dist_sq = jnp.maximum(dx * dx + dy * dy + dz * dz, TINY)
    inverse = lax.rsqrt(dist_sq)
    radius = dist_sq * inverse
    slope = (slope_part(radius, row[6], row[7]) + slope_part(radius, lane[6], lane[7])) * inverse
    approach = (lane[3] - row[3]) * dx + (lane[4] - row[4]) * dy + (lane[5] - row[5]) * dz
    smooth = lane[11] + row[11]
    converge = (
        smooth * jnp.minimum(approach, 0.0) * pl.reciprocal(dist_sq + smooth * smooth, approx=True)
    )
    viscous = converge * (converge - (lane[8] + row[8])) * pl.reciprocal(lane[9] + row[9], approx=True)
    lane_term = lane[10] + viscous
    row_term = row[10] + viscous
    return dx, dy, dz, slope, approach, lane_term, row_term


def spread_force(table, extra, held, cell, count):
    rows = [(i, cell_row(table, cell, r)) for i, r in enumerate((0, 1, 2, 5, 6, 7))]
    rows += [(6 + i, cell_row(extra, cell, i)) for i in range(6)]
    rows += [(12, cell_row(table, cell, 3))]
    spread(rows, held, count)


def force_rows_pass(held, trips, lanes, lane_fields, add_lane, row_sums):
    size = FORCE_ROWS

    def chunk(step, totals):
        rows = pl.ds(pl.multiple_of(step * size, size), size)
        row = [held[i, rows, :] for i in range(13)]
        result = []
        row_total = None
        if row_sums is not None:
            row_total = [row_sums[i, rows, :] for i in range(4)]
        for index, lane in enumerate(lane_fields):
            dx, dy, dz, slope, approach, lane_term, row_term = force_pair(row, lane)
            common = lane_term + row_term
            weight = row[12] * slope
            pull = weight * common
            terms = (pull * dx, pull * dy, pull * dz, weight * approach * lane_term)
            result += [t + summed_rows(v) for t, v in zip(totals[4 * index :], terms)]
            if row_sums is not None:
                weight = lane[12] * slope
                pull = weight * common
                terms = (pull * dx, pull * dy, pull * dz, weight * approach * row_term)
                row_total = [t + v for t, v in zip(row_total, terms)]
        if row_sums is not None:
            for i in range(4):
                row_sums[i, rows, :] = row_total[i]
        return tuple(result)

    totals = lax.fori_loop(0, trips, chunk, (jnp.zeros((8, 128), F32),) * (4 * len(lanes)))
    for index, l in enumerate(lanes):
        add_lane(l, [jnp.sum(t, axis=0, keepdims=True) for t in totals[4 * index : 4 * index + 4]])


def add_to(sums, cell):
    def add_lane(l, parts):
        for i, part in enumerate(parts):
            sums[cell, i : i + 1, l : l + 128] += part

    return add_lane


def force_local_kernel(counts, starts, listed, table, raw, own, extra, held):
    own[...] = jnp.zeros_like(own)
    local_force_fields(table, raw, extra)

    def per_cell(cell, carry):
        count = counts[cell]
        spread_force(table, extra, held, cell, count)
        trips = (count + (FORCE_ROWS - 1)) // FORCE_ROWS

        def pair(target):
            def block(lanes):
                fields = []
                for l in lanes:
                    part = [table[target, i : i + 1, l : l + 128] for i in (0, 1, 2, 5, 6, 7)]
                    fields.append(part + [extra[target, i : i + 1, l : l + 128] for i in range(6)])
                force_rows_pass(held, trips, lanes, fields, add_to(own, target), None)

            by_width(counts[target] > 128, block)

        pair(cell)
        lax.fori_loop(starts[cell], starts[cell + 1], lambda j, c: (pair(listed[j]), c)[1], 0)
        return carry

    lax.fori_loop(0, CELLS, per_cell, 0)


def force_cross_kernel(
    counts, starts, listed, wide, table, raw, n5, n6, n7, n8, f5, f6, f7, f8, l5, l6, l7, l8,
    own, b5, b6, b7, b8, extra, near, far, late, held, row_sums, back,
):
    own[...] = jnp.zeros_like(own)
    back[...] = jnp.zeros_like(back)
    local_force_fields(table, raw, extra)
    for direction, (n, f, l) in enumerate(((n5, f5, l5), (n6, f6, l6), (n7, f7, l7), (n8, f8, l8))):
        near[direction * EXPORT : (direction + 1) * EXPORT] = n[...]
        far[direction * EXPORT : (direction + 1) * EXPORT] = f[...]

        def one(k, carry):
            slot = direction * EXPORT + k
            force_fields(late, slot, f[k, 0:1, :], l[k, 0:1, :], l[k, 1:2, :])
            return carry

        lax.fori_loop(0, EXPORT, one, 0)

    def per_cell(cell, carry):
        count = counts[cell]

        @pl.when(starts[cell + 1] > starts[cell])
        def with_pairs():
            spread_force(table, extra, held, cell, count)
            trips = (count + (FORCE_ROWS - 1)) // FORCE_ROWS
            row_sums[...] = jnp.zeros_like(row_sums)

            def pair(source):
                def block(lanes):
                    fields = []
                    for l in lanes:
                        part = [near[source, i : i + 1, l : l + 128] for i in (0, 1, 2)]
                        part += [far[source, i : i + 1, l : l + 128] for i in (1, 2, 3)]
                        part += [late[source, i : i + 1, l : l + 128] for i in range(6)]
                        fields.append(part + [near[source, 3:4, l : l + 128]])
                    force_rows_pass(held, trips, lanes, fields, add_to(back, source), row_sums)

                by_width(wide[source] > 0, block)

            lax.fori_loop(starts[cell], starts[cell + 1], lambda j, c: (pair(listed[j]), c)[1], 0)
            for i in range(4):
                for l in (0, 128):
                    flipped = jnp.transpose(row_sums[i, l : l + 128, :])
                    total = jnp.sum(flipped, axis=0, keepdims=True)
                    own[cell, i : i + 1, l : l + 128] = total if i == 3 else -total

        return carry

    lax.fori_loop(0, CELLS, per_cell, 0)
    for direction, out in enumerate((b5, b6, b7, b8)):
        out[...] = back[direction * EXPORT : (direction + 1) * EXPORT]


def finish_kernel(exports, table, raw, first, second, r0, r1, r2, density, acceleration, rate, total):
    total[...] = first[...] + second[...]

    def add(k, carry):
        total[exports[k]] += r0[k] + r1[k] + r2[k]
        return carry

    lax.fori_loop(0, EXPORT, add, 0)
    for cell in range(CELLS):
        one = slice(cell, cell + 1)
        live = table[cell, 9:10, :]
        density[one, :] = raw[cell] * live
        for axis in range(3):
            acceleration[axis, one, :] = total[cell, axis : axis + 1, :] * live
        rate[one, :] = -total[cell, 3:4, :] * live


def shape(*dims):
    return jax.ShapeDtypeStruct(dims, F32)


def call(kernel, out, scalars, arrays, scratch, flops):
    many = isinstance(out, (list, tuple))
    count = len(out) if many else 1
    specs = [pl.BlockSpec(memory_space=VMEM)] * count
    return pl.pallas_call(
        kernel,
        out_shape=out,
        in_specs=[pl.BlockSpec(memory_space=SMEM)] * len(scalars)
        + [pl.BlockSpec(memory_space=VMEM)] * len(arrays),
        out_specs=specs if many else specs[0],
        scratch_shapes=scratch,
        compiler_params=pltpu.CompilerParams(vmem_limit_bytes=40 << 20),
        cost_estimate=pl.CostEstimate(flops=flops, bytes_accessed=2 << 20, transcendentals=0),
    )(*scalars, *arrays)


def shifted(block, axis, distance):
    count = lax.axis_size(axis)
    return lax.ppermute(block, axis, [((i - distance) % count, i) for i in range(count)])


def grouped(keys, values):
    index = jnp.arange(keys.shape[0], dtype=jnp.int32)
    ahead = (keys[None, :] < keys[:, None]) | (
        (keys[None, :] == keys[:, None]) & (index[None, :] < index[:, None])
    )
    place = jnp.sum(ahead.astype(jnp.int32), axis=1)
    ordered = jnp.sum(jnp.where(place[None, :] == index[:, None], values[None, :], 0), axis=1)
    cells = jnp.arange(CELLS + 1, dtype=jnp.int32)
    starts = jnp.sum((keys[None, :] < cells[:, None]).astype(jnp.int32), axis=1)
    return starts, ordered


def body(pos, vel, energy, masses, bins, counts, exports, cross_pairs, local_pairs):
    upper = cross_pairs.shape[1] // 2
    local_starts, local_list = grouped(local_pairs[1], local_pairs[0])
    cross_starts, cross_list = grouped(cross_pairs[0], cross_pairs[1])
    upper_starts, upper_list = grouped(cross_pairs[0, :upper], cross_pairs[1, :upper] - 5 * EXPORT)
    table, near, far = call(
        prepare_kernel,
        [shape(CELLS, 16, SLOTS), shape(EXPORT, 4, SLOTS), shape(EXPORT, 4, SLOTS)],
        [counts, exports],
        [pos, vel, energy, masses, bins],
        [],
        1 << 20,
    )
    down, up = shifted(near, "gx", 1), shifted(near, "gx", -1)
    left, right = shifted(near, "yz", 1), shifted(near, "yz", -1)
    near_blocks = {
        1: down, 7: up, 3: left, 5: right,
        0: shifted(down, "yz", 1), 2: shifted(down, "yz", -1),
        6: shifted(up, "yz", 1), 8: shifted(up, "yz", -1),
    }

    def upper_blocks(block):
        above = shifted(block, "gx", -1)
        return [shifted(block, "yz", -1), shifted(above, "yz", 1), above, shifted(above, "yz", -1)]

    far_blocks = upper_blocks(far)
    partial = call(
        density_local_kernel,
        shape(CELLS, 1, SLOTS),
        [counts, local_starts, local_list],
        [table],
        [VMEM((4, SLOTS, 128), F32)],
        1 << 30,
    )
    ordered = [near_blocks[i] for i in (0, 1, 2, 3, 5, 6, 7, 8)]
    wide = jnp.concatenate(
        [b[:, 3, 128] for b in ordered[:4]]
        + [jnp.zeros((EXPORT,), F32)]
        + [b[:, 3, 128] for b in ordered[4:]]
    )
    wide = (wide > 0).astype(jnp.int32)
    raw, late = call(
        density_cross_kernel,
        [shape(CELLS, 1, SLOTS), shape(EXPORT, 2, SLOTS)],
        [counts, exports, cross_starts, cross_list, wide],
        [table, partial] + ordered,
        [VMEM((9 * EXPORT, 4, SLOTS), F32), VMEM((4, SLOTS, 128), F32), VMEM((SLOTS, 128), F32)],
        2 << 30,
    )
    late_blocks = upper_blocks(late)
    first = call(
        force_local_kernel,
        shape(CELLS, 4, SLOTS),
        [counts, local_starts, local_list],
        [table, raw],
        [VMEM((CELLS, 8, SLOTS), F32), VMEM((13, SLOTS, 128), F32)],
        3 << 30,
    )
    second, right_back, left_back, up_back, corner_back = call(
        force_cross_kernel,
        [shape(CELLS, 4, SLOTS)] + [shape(EXPORT, 4, SLOTS)] * 4,
        [counts, upper_starts, upper_list, wide[5 * EXPORT :]],
        [table, raw] + [near_blocks[i] for i in (5, 6, 7, 8)] + far_blocks + late_blocks,
        [
            VMEM((CELLS, 8, SLOTS), F32),
            VMEM((4 * EXPORT, 4, SLOTS), F32),
            VMEM((4 * EXPORT, 4, SLOTS), F32),
            VMEM((4 * EXPORT, 8, SLOTS), F32),
            VMEM((13, SLOTS, 128), F32),
            VMEM((4, SLOTS, 128), F32),
            VMEM((4 * EXPORT, 4, SLOTS), F32),
        ],
        3 << 30,
    )
    from_below = shifted(up_back, "gx", 1)
    from_right = shifted(shifted(left_back, "gx", 1), "yz", -1)
    from_left = shifted(right_back + shifted(corner_back, "gx", 1), "yz", 1)
    return call(
        finish_kernel,
        [shape(CELLS, SLOTS), shape(3, CELLS, SLOTS), shape(CELLS, SLOTS)],
        [exports],
        [table, raw, first, second, from_below, from_right, from_left],
        [VMEM((CELLS, 4, SLOTS), F32)],
        1 << 20,
    )


def solution(mesh):
    both = ("gx", "yz")
    return jax.shard_map(
        body,
        mesh=mesh,
        in_specs=(
            P(None, both, None),
            P(None, both, None),
            P(both, None),
            P(both, None),
            P(both, None),
            P(both),
            P(both),
            P(None, both),
            P(None, both),
        ),
        out_specs=(P(both, None), P(None, both, None), P(both, None)),
        check_vma=False,
    )
```

```python
import math

import jax
import jax.numpy as jnp
from jax import lax
from jax.experimental import pallas as pl
from jax.experimental.pallas import tpu as pltpu
from jax.sharding import PartitionSpec as P

F32, I32 = jnp.float32, jnp.int32
SIGMA_NORM = 0.3183098861837907
GAMMA_GAS = 5.0 / 3.0
TINY = 1e-24
CELLS, SLOTS, EXPORT = 64, 256, 32
PIECES = 2
DENSITY_ROWS = 64
FORCE_ROWS = 32
SHARE = 24
ROOT = math.sqrt(1.5 * SIGMA_NORM)
VMEM, SMEM = pltpu.VMEM, pltpu.SMEM
MESH = pl.DeviceIdType.MESH
SIDES = (0, 1, 2, 3, 5, 6, 7, 8)
FORCE_LANES = [(0, 0), (0, 1), (0, 2), (0, 5), (0, 6), (0, 7), (1, 0), (1, 1), (1, 2), (2, 0), (2, 1), (1, 3), (0, 3)]
FORCE_FAR = [(0, 0), (0, 1), (0, 2), (0, 5), (0, 6), (0, 7), (1, 0), (1, 1), (1, 2), (1, 4), (1, 5), (1, 3), (0, 3)]


def by_width(flag, block):
    @pl.when(flag)
    def wide_block():
        block((0, 128))

    @pl.when(jnp.logical_not(flag))
    def narrow_block():
        block((0,))


def flipped(row):
    return jnp.transpose(jnp.broadcast_to(row, (128, 128)))


def spread(rows, target, count, derive=None):
    def half(start):
        made = {}
        for slot, table, cell, row in rows:
            made[slot] = flipped(table[cell, row : row + 1, start : start + 128])
        if derive is not None:
            derive(made)
        for slot, value in made.items():
            target[slot, start : start + 128, :] = value

    half(0)

    @pl.when(count > 128)
    def second_half():
        half(128)


def summed_rows(values):
    return jnp.sum(values.reshape(values.shape[0] // 8, 8, 128), axis=0)


def spline_unscaled(radius, smooth_twice, smooth):
    outer = jnp.maximum(smooth_twice - radius, 0.0)
    inner = jnp.maximum(smooth - radius, 0.0)
    return (0.25 * outer) * (outer * outer) - inner * (inner * inner)


def prepare_kernel(counts, exports, pos, vel, energy, masses, bins, first, second, near, far):
    lane = lax.broadcasted_iota(I32, (1, SLOTS), 1)
    smooth = 0.4 * jnp.exp2(bins[...].astype(F32) * math.log2(1.2))
    made = derived_fields(smooth, energy[...])
    for cell in range(CELLS):
        live = (lane < counts[cell]).astype(F32)
        one = slice(cell, cell + 1)
        for axis in range(3):
            first[cell, axis : axis + 1, :] = pos[axis, one, :]
            first[cell, 5 + axis : 6 + axis, :] = vel[axis, one, :]
        first[cell, 3:4, :] = masses[one, :] * live
        first[cell, 4:5, :] = smooth[one, :]
        for i, value in enumerate(made):
            second[cell, i : i + 1, :] = value[one, :]
        second[cell, 4:5, :] = energy[one, :]
        second[cell, 5:6, :] = live

    def gather(k, carry):
        near[k] = first[exports[k]]
        far[k] = second[exports[k], 4:5, :]
        return carry

    lax.fori_loop(0, EXPORT, gather, 0)


def derived_fields(smooth, energy):
    inverse = pl.reciprocal(smooth, approx=True)
    square = inverse * inverse
    sound = jnp.sqrt(GAMMA_GAS * (GAMMA_GAS - 1.0) * energy) * (1.0 / 40.0)
    return (0.5 * ROOT) * (square * inverse), ROOT * square, sound, 0.05 * smooth


def place_of(side):
    rows, columns = lax.axis_size("gx"), lax.axis_size("yz")
    g = lax.rem(lax.axis_index("gx") + (side // 3 - 1 + rows), rows)
    y = lax.rem(lax.axis_index("yz") + (side % 3 - 1 + columns), columns)
    return g, y


def greet(sides):
    barrier = pltpu.get_barrier_semaphore()
    for side in sides:
        pl.semaphore_signal(barrier, inc=1, device_id=place_of(side), device_id_type=MESH)
    pl.semaphore_wait(barrier, len(sides))


def remote(source, target, send, receive, side):
    return pltpu.make_async_remote_copy(
        src_ref=source,
        dst_ref=target,
        send_sem=send,
        recv_sem=receive,
        device_id=place_of(side),
        device_id_type=MESH,
    )


def part_of(ref, side, piece):
    size = EXPORT // PIECES
    return ref.at[pl.ds(side * EXPORT + piece * size, size)]


def halo_kernel(near, far, note, near_all, far_all, notes, send, receive):
    greet((1, 3, 5, 7))
    kinds = [(near, near_all, p) for p in range(PIECES)] + [(far, far_all, None), (note, notes, None)]
    started = {}

    def view(ref, slot, piece):
        if piece is not None:
            return part_of(ref, slot, piece)
        size = EXPORT if ref is far_all or ref is far else 1
        return ref.at[pl.ds(slot * size, size)]

    for kind, (own, whole, piece) in enumerate(kinds):
        for side in (7, 1, 5, 3):
            slot = 8 - side
            copy = remote(view(own, 0, piece), view(whole, slot, piece), send.at[kind, slot], receive.at[kind, slot], side)
            copy.start()
            started[kind, slot] = copy
    for kind, (own, whole, piece) in enumerate(kinds):
        for came in (1, 7):
            started[kind, came].wait_recv()
            for side in (5, 3):
                slot = came + (-1 if side == 5 else 1)
                copy = remote(view(whole, came, piece), view(whole, slot, piece), send.at[kind, slot], receive.at[kind, slot], side)
                copy.start()
                started[kind, slot] = copy
    for (kind, slot), copy in started.items():
        copy.wait_send()
        if slot not in (1, 7):
            copy.wait_recv()


def swap_all(source, target, send, receive, stride):
    copies = []
    for side in SIDES:
        slot = 8 - side
        piece = source.at[pl.ds(side * EXPORT, EXPORT)] if stride else source
        copy = remote(piece, target.at[pl.ds(slot * EXPORT, EXPORT)], send.at[slot], receive.at[slot], side)
        copy.start()
        copies.append(copy)
    for copy in copies:
        copy.wait()


def total_of(block):
    parts = [block[side * EXPORT : (side + 1) * EXPORT] for side in SIDES]
    return ((parts[0] + parts[1]) + (parts[2] + parts[3])) + ((parts[4] + parts[5]) + (parts[6] + parts[7]))


def combine_kernel(exports, slot_of, first, second, partial, back, raw, late, late_all, came, sent, total, send, receive):
    greet(SIDES)
    swap_all(back, came, send.at[0], receive.at[0], True)
    total[...] = total_of(came)

    def per_cell(cell, carry):
        slot = slot_of[cell]
        extra = jnp.where(slot >= 0, total[jnp.maximum(slot, 0)], 0.0)
        inverse = pl.reciprocal(first[cell, 4:5, :], approx=True)
        cube = inverse * inverse * inverse
        value = (partial[cell] + extra) * (SIGMA_NORM * cube * cube)
        raw[cell] = value
        rho = jnp.where(second[cell, 5:6, :] > 0, value, 1.0)
        late[cell, 0:1, :] = rho * (1.0 / 200.0)
        late[cell, 1:2, :] = (GAMMA_GAS - 1.0) * second[cell, 4:5, :] * pl.reciprocal(rho, approx=True)
        return carry

    lax.fori_loop(0, CELLS, per_cell, 0)

    def gather(k, carry):
        sent[k] = late[exports[k], 0:1, :]
        return carry

    lax.fori_loop(0, EXPORT, gather, 0)
    swap_all(sent, late_all, send.at[1], receive.at[1], False)


def return_kernel(back, came, send, receive):
    greet(SIDES)
    swap_all(back, came, send, receive, True)


def lower_share(lower, upper):
    both = lower + upper
    scaled = jnp.maximum(2 * SHARE * (upper - lower) + (EXPORT + 1) * both, 0)
    return jnp.minimum(lax.div(scaled, 2 * both), EXPORT)


def set_shares(notes, shares):
    mine = notes[4, EXPORT]
    for side in SIDES:
        other = notes[side, EXPORT]
        shares[side] = lower_share(mine, other) if side > 4 else lower_share(other, mine)


def cross_loop(starts, listed, shares, notes, cell, slot, work):
    def one(j, carry):
        source = listed[j]
        side, place = source // EXPORT, source % EXPORT
        share = shares[side]
        active = jnp.where(side > 4, (place < share).astype(I32), (slot >= share).astype(I32))

        @pl.when(active > 0)
        def with_source():
            by_width(notes[side, place] > 128, lambda lanes: work(source, lanes))

        return carry

    lax.fori_loop(starts[cell], starts[cell + 1], one, 0)


def density_lanes(held, count, table, target, lanes, add_lane, lane_mass, row_sums):
    size = DENSITY_ROWS
    trips = (count + (size - 1)) // size
    fields = []
    for l in lanes:
        x, y, z, m, h = (table[target, i : i + 1, l : l + 128] for i in range(5))
        fields.append((x, y, z, m, h, h + h))

    def chunk(step, totals):
        rows = pl.ds(pl.multiple_of(step * size, size), size)
        rx, ry, rz, mass = (held[i, rows, :] for i in range(4))
        if lane_mass:
            rh = held[4, rows, :]
            rh2 = rh + rh
            row_total = row_sums[rows, :]
        result = []
        for total, (x, y, z, m, h1, h2) in zip(totals, fields):
            dx, dy, dz = x - rx, y - ry, z - rz
            dist_sq = jnp.maximum(dx * dx + dy * dy + dz * dz, TINY)
            radius = dist_sq * lax.rsqrt(dist_sq)
            result.append(total + summed_rows(spline_unscaled(radius, h2, h1) * mass))
            if lane_mass:
                row_total = row_total + spline_unscaled(radius, rh2, rh) * m
        if lane_mass:
            row_sums[rows, :] = row_total
        return tuple(result)

    totals = lax.fori_loop(0, trips, chunk, (jnp.zeros((8, 128), F32),) * len(lanes))
    for l, total in zip(lanes, totals):
        add_lane[target, :, l : l + 128] += jnp.sum(total, axis=0, keepdims=True)


def density_local(counts, starts, listed, table, raw, held, cell, count):
    def pair(target):
        by_width(
            counts[target] > 128,
            lambda lanes: density_lanes(held, count, table, target, lanes, raw, False, None),
        )

    pair(cell)
    lax.fori_loop(starts[cell], starts[cell + 1], lambda j, c: (pair(listed[j]), c)[1], 0)


def density_kernel(
    counts, slot_of, starts, listed, cross_starts, cross_list, notes, table, imports,
    raw, back, held, sums, shares,
):
    raw[...] = jnp.zeros_like(raw)
    back[...] = jnp.zeros_like(back)
    set_shares(notes, shares)

    def per_cell(cell, carry):
        count = counts[cell]
        slot = slot_of[cell]
        spread([(i, table, cell, i) for i in range(5)], held, count)
        density_local(counts, starts, listed, table, raw, held, cell, count)

        @pl.when(slot >= 0)
        def with_pairs():
            sums[...] = jnp.zeros_like(sums)
            cross_loop(
                cross_starts, cross_list, shares, notes, cell, slot,
                lambda source, lanes: density_lanes(
                    held, count, imports, source, lanes, back, True, sums
                ),
            )
            for l in (0, 128):
                turned = jnp.transpose(sums[l : l + 128, :])
                raw[cell, :, l : l + 128] += jnp.sum(turned, axis=0, keepdims=True)

        return carry

    lax.fori_loop(0, CELLS, per_cell, 0)


def slope_part(radius, half_beta, beta_h):
    reach = half_beta * radius
    outer = jnp.maximum(beta_h - reach, 0.0)
    least = jnp.minimum(outer, reach)
    return least * (outer + (outer - least))


def force_pair(row, lane):
    dx, dy, dz = lane[0] - row[0], lane[1] - row[1], lane[2] - row[2]
    dist_sq = jnp.maximum(dx * dx + dy * dy + dz * dz, TINY)
    inverse = lax.rsqrt(dist_sq)
    radius = dist_sq * inverse
    slope = (slope_part(radius, row[6], row[7]) + slope_part(radius, lane[6], lane[7])) * inverse
    approach = (lane[3] - row[3]) * dx + (lane[4] - row[4]) * dy + (lane[5] - row[5]) * dz
    smooth = lane[11] + row[11]
    converge = (
        smooth * jnp.minimum(approach, 0.0) * pl.reciprocal(dist_sq + smooth * smooth, approx=True)
    )
    viscous = converge * (converge - (lane[8] + row[8])) * pl.reciprocal(lane[9] + row[9], approx=True)
    lane_term = lane[10] + viscous
    row_term = row[10] + viscous
    return dx, dy, dz, slope, approach, lane_term, row_term


def spread_force(tables, held, cell, count):
    rows = [(i, tables[t], cell, r) for i, (t, r) in enumerate(FORCE_LANES) if i not in (6, 7, 10, 11)]
    rows.append((13, tables[0], cell, 4))

    def derive(made):
        smooth = made.pop(13)
        inverse = pl.reciprocal(smooth, approx=True)
        square = inverse * inverse
        made[7] = ROOT * square
        made[6] = (0.5 * ROOT) * (square * inverse)
        made[11] = 0.05 * smooth
        made[10] = 4.8 * (made[8] * made[8]) * pl.reciprocal(made[9], approx=True)

    spread(rows, held, count, derive)


def force_lanes(held, count, tables, target, lanes, add_lane, row_sums, places):
    size = FORCE_ROWS
    trips = (count + (size - 1)) // size
    fields = [[tables[t][target, i : i + 1, l : l + 128] for t, i in places] for l in lanes]

    def chunk(step, totals):
        rows = pl.ds(pl.multiple_of(step * size, size), size)
        row = [held[i, rows, :] for i in range(13)]
        result = []
        if row_sums is not None:
            row_total = [row_sums[i, rows, :] for i in range(4)]
        for index, lane in enumerate(fields):
            dx, dy, dz, slope, approach, lane_term, row_term = force_pair(row, lane)
            common = lane_term + row_term
            weight = row[12] * slope
            pull = weight * common
            terms = (pull * dx, pull * dy, pull * dz, weight * approach * lane_term)
            result += [t + summed_rows(v) for t, v in zip(totals[4 * index :], terms)]
            if row_sums is not None:
                weight = lane[12] * slope
                pull = weight * common
                terms = (pull * dx, pull * dy, pull * dz, weight * approach * row_term)
                row_total = [t + v for t, v in zip(row_total, terms)]
        if row_sums is not None:
            for i in range(4):
                row_sums[i, rows, :] = row_total[i]
        return tuple(result)

    totals = lax.fori_loop(0, trips, chunk, (jnp.zeros((8, 128), F32),) * (4 * len(lanes)))
    for index, l in enumerate(lanes):
        for i in range(4):
            part = jnp.sum(totals[4 * index + i], axis=0, keepdims=True)
            add_lane[target, i : i + 1, l : l + 128] += part


def force_local(counts, starts, listed, tables, own, held, cell, count):
    def pair(target):
        by_width(
            counts[target] > 128,
            lambda lanes: force_lanes(held, count, tables, target, lanes, own, None, FORCE_LANES),
        )

    pair(cell)
    lax.fori_loop(starts[cell], starts[cell + 1], lambda j, c: (pair(listed[j]), c)[1], 0)


def force_kernel(
    counts, slot_of, starts, listed, cross_starts, cross_list, notes,
    first, second, late, imports, energies, densities,
    own, back, derived, held, row_sums, shares,
):
    own[...] = jnp.zeros_like(own)
    back[...] = jnp.zeros_like(back)
    set_shares(notes, shares)
    for side in SIDES:

        def derive(step, carry):
            cells = pl.ds(side * EXPORT + step * 8, 8)
            energy = energies[cells, 0, :]
            rho = densities[cells, 0, :]
            made = derived_fields(imports[cells, 4, :], energy)
            press = (GAMMA_GAS - 1.0) / 200.0 * energy * pl.reciprocal(rho, approx=True)
            for i, value in enumerate(made + (rho, press)):
                derived[cells, i, :] = value
            return carry

        lax.fori_loop(0, EXPORT // 8, derive, 0)
    tables = (first, second, late)
    far_tables = (imports, derived)

    def per_cell(cell, carry):
        count = counts[cell]
        slot = slot_of[cell]
        spread_force(tables, held, cell, count)
        force_local(counts, starts, listed, tables, own, held, cell, count)

        @pl.when(slot >= 0)
        def with_pairs():
            row_sums[...] = jnp.zeros_like(row_sums)
            cross_loop(
                cross_starts, cross_list, shares, notes, cell, slot,
                lambda source, lanes: force_lanes(
                    held, count, far_tables, source, lanes, back, row_sums, FORCE_FAR
                ),
            )

            def finish(l):
                for i in range(4):
                    turned = jnp.transpose(row_sums[i, l : l + 128, :])
                    total = jnp.sum(turned, axis=0, keepdims=True)
                    own[cell, i : i + 1, l : l + 128] += total if i == 3 else -total

            finish(0)

            @pl.when(count > 128)
            def second_half():
                finish(128)

        return carry

    lax.fori_loop(0, CELLS, per_cell, 0)


def finish_kernel(exports, second, raw, own, came, density, acceleration, rate, extra, total):
    extra[...] = total_of(came)
    total[...] = own[...]

    def add(k, carry):
        total[exports[k]] += extra[k]
        return carry

    lax.fori_loop(0, EXPORT, add, 0)
    for cell in range(CELLS):
        one = slice(cell, cell + 1)
        live = second[cell, 5:6, :]
        density[one, :] = raw[cell] * live
        for axis in range(3):
            acceleration[axis, one, :] = total[cell, axis : axis + 1, :] * live
        rate[one, :] = -total[cell, 3:4, :] * live


def shape(*dims):
    return jax.ShapeDtypeStruct(dims, F32)


def call(kernel, out, scalars, arrays, scratch, limit=40, collective=None):
    many = isinstance(out, (list, tuple))
    count = len(out) if many else 1
    specs = [pl.BlockSpec(memory_space=VMEM)] * count
    extra = {} if collective is None else dict(collective_id=collective, has_side_effects=True)
    return pl.pallas_call(
        kernel,
        out_shape=out,
        in_specs=[pl.BlockSpec(memory_space=SMEM)] * len(scalars)
        + [pl.BlockSpec(memory_space=VMEM)] * len(arrays),
        out_specs=specs if many else specs[0],
        scratch_shapes=scratch,
        compiler_params=pltpu.CompilerParams(vmem_limit_bytes=limit << 20, **extra),
    )(*scalars, *arrays)


def grouped(keys, values):
    index = jnp.arange(keys.shape[0], dtype=I32)
    ahead = (keys[None, :] < keys[:, None]) | (
        (keys[None, :] == keys[:, None]) & (index[None, :] < index[:, None])
    )
    place = jnp.sum(ahead.astype(I32), axis=1)
    ordered = jnp.sum(jnp.where(place[None, :] == index[:, None], values[None, :], 0), axis=1)
    cells = jnp.arange(CELLS + 1, dtype=I32)
    starts = jnp.sum((keys[None, :] < cells[:, None]).astype(I32), axis=1)
    return starts, ordered


def body(pos, vel, energy, masses, bins, counts, exports, cross_pairs, local_pairs):
    cell_ids = jnp.arange(CELLS, dtype=I32)
    slots = jnp.arange(EXPORT, dtype=I32)
    is_export = exports[None, :] == cell_ids[:, None]
    load = jnp.sum(counts * counts)
    export_counts = jnp.sum(jnp.where(is_export, counts[:, None], 0), axis=0)
    note = jnp.concatenate([export_counts, jnp.broadcast_to(load, (128 - EXPORT,))])
    slot_of = jnp.sum(jnp.where(is_export, slots[None, :] + 1, 0), axis=1) - 1
    local_starts, local_list = grouped(local_pairs[1], local_pairs[0])
    cross_starts, cross_list = grouped(cross_pairs[0], cross_pairs[1])
    sems = pltpu.SemaphoreType.DMA
    first, second, near, far = call(
        prepare_kernel,
        [shape(CELLS, 8, SLOTS), shape(CELLS, 8, SLOTS), shape(EXPORT, 8, SLOTS), shape(EXPORT, 1, SLOTS)],
        [counts, exports],
        [pos, vel, energy, masses, bins],
        [],
        60,
    )
    imports, energies, notes = call(
        halo_kernel,
        [
            shape(9 * EXPORT, 8, SLOTS),
            shape(9 * EXPORT, 1, SLOTS),
            jax.ShapeDtypeStruct((9, 1, 128), I32),
        ],
        [],
        [near, far, note[None, None]],
        [sems((PIECES + 2, 9)), sems((PIECES + 2, 9))],
        40,
        0,
    )
    notes = jnp.concatenate([notes[:4, 0], note[None], notes[5:, 0]])
    lists = [local_starts, local_list, cross_starts, cross_list, notes]
    partial, back = call(
        density_kernel,
        [shape(CELLS, 1, SLOTS), shape(9 * EXPORT, 1, SLOTS)],
        [counts, slot_of] + lists,
        [first, imports],
        [VMEM((5, SLOTS, 128), F32), VMEM((SLOTS, 128), F32), SMEM((16,), I32)],
    )
    raw, late, densities = call(
        combine_kernel,
        [shape(CELLS, 1, SLOTS), shape(CELLS, 2, SLOTS), shape(9 * EXPORT, 1, SLOTS)],
        [exports, slot_of],
        [first, second, partial, back],
        [
            VMEM((9 * EXPORT, 1, SLOTS), F32),
            VMEM((EXPORT, 1, SLOTS), F32),
            VMEM((EXPORT, 1, SLOTS), F32),
            sems((2, 9)),
            sems((2, 9)),
        ],
        40,
        1,
    )
    own, back = call(
        force_kernel,
        [shape(CELLS, 4, SLOTS), shape(9 * EXPORT, 4, SLOTS)],
        [counts, slot_of] + lists,
        [first, second, late, imports, energies, densities],
        [
            VMEM((9 * EXPORT, 8, SLOTS), F32),
            VMEM((13, SLOTS, 128), F32),
            VMEM((4, SLOTS, 128), F32),
            SMEM((16,), I32),
        ],
    )
    came = call(
        return_kernel,
        shape(9 * EXPORT, 4, SLOTS),
        [],
        [back],
        [sems((9,)), sems((9,))],
        40,
        2,
    )
    return tuple(
        call(
            finish_kernel,
            [shape(CELLS, SLOTS), shape(3, CELLS, SLOTS), shape(CELLS, SLOTS)],
            [exports],
            [second, raw, own, came],
            [VMEM((EXPORT, 4, SLOTS), F32), VMEM((CELLS, 4, SLOTS), F32)],
        )
    )


def solution(mesh):
    both = ("gx", "yz")
    return jax.shard_map(
        body,
        mesh=mesh,
        in_specs=(
            P(None, both, None),
            P(None, both, None),
            P(both, None),
            P(both, None),
            P(both, None),
            P(both),
            P(both),
            P(None, both),
            P(None, both),
        ),
        out_specs=(P(both, None), P(None, both, None), P(both, None)),
        check_vma=False,
    )
```

```python
import math

import jax
import jax.numpy as jnp
from jax import lax
from jax.experimental import pallas as pl
from jax.experimental.pallas import tpu as pltpu
from jax.sharding import PartitionSpec as P

F32, I32 = jnp.float32, jnp.int32
SIGMA_NORM = 0.3183098861837907
GAMMA_GAS = 5.0 / 3.0
TINY = 1e-24
CELLS, SLOTS, EXPORT = 64, 256, 32
PIECES = 2
TOGETHER = 4
COUNTS, SLOT_OF, EXPORTS, LOCAL_STARTS, LOCAL_LIST, CROSS_STARTS, CROSS_LIST = 0, 64, 128, 160, 232, 296, 368
LOCAL_FIRST, CROSS_FIRST, PLAN_COUNTS, PLAN_SLOTS, LOCAL_TILES, CROSS_TILES, PLAN_SIZE = 0, 72, 144, 208, 272, 536, 1088
DENSITY_ROWS = 64
FORCE_ROWS = 32
ROOT = math.sqrt(1.5 * SIGMA_NORM)
VMEM, SMEM = pltpu.VMEM, pltpu.SMEM
MESH = pl.DeviceIdType.MESH
SIDES = (0, 1, 2, 3, 5, 6, 7, 8)
FORCE_LANES = [(0, 0), (0, 1), (0, 2), (0, 5), (0, 6), (0, 7), (1, 0), (1, 1), (1, 2), (2, 0), (2, 1), (1, 3), (0, 3)]
FORCE_FAR = [(0, 0), (0, 1), (0, 2), (0, 5), (0, 6), (0, 7), (1, 0), (1, 1), (1, 2), (1, 4), (1, 5), (1, 3), (0, 3)]


def over_tiles(plan, start, count, block):
    def tile(index):
        entry = plan[start + index]
        return entry // 2, pl.ds(pl.multiple_of((entry % 2) * 128, 128), 128)

    def two(step, carry):
        block((tile(2 * step), tile(2 * step + 1)))
        return carry

    lax.fori_loop(0, count // 2, two, 0)

    @pl.when(count % 2 == 1)
    def last():
        block((tile(count - 1),))


def over_part(plan, cell, firsts, tiles, block):
    start = plan[firsts + cell]
    over_tiles(plan, tiles + start, plan[firsts + cell + 1] - start, block)


def flipped(row):
    return jnp.transpose(jnp.broadcast_to(row, (128, 128)))


def spread(rows, target, cells, counts, size, derive=None):
    def half(place, cell, start):
        made = {}
        for slot, table, row in rows:
            made[slot] = flipped(table[cell, row : row + 1, start : start + 128])
        if derive is not None:
            derive(made)
        for slot, value in made.items():
            target[place * size + slot, start : start + 128, :] = value

    for place, cell in enumerate(cells):
        half(place, cell, 0)
    for place, cell in enumerate(cells):

        @pl.when(counts[place] > 128)
        def second_half():
            half(place, cell, 128)


def over_cells(plan, lay, work):
    def group(step, carry):
        cells = [step * TOGETHER + i for i in range(TOGETHER)]
        lay(cells, [plan[PLAN_COUNTS + cell] for cell in cells])
        lax.fori_loop(0, TOGETHER, lambda i, c: (work(step * TOGETHER + i, i), c)[1], 0)
        return carry

    lax.fori_loop(0, CELLS // TOGETHER, group, 0)


def summed_rows(values):
    return jnp.sum(values.reshape(values.shape[0] // 8, 8, 128), axis=0)


def spline_unscaled(radius, smooth_twice, smooth):
    outer = jnp.maximum(smooth_twice - radius, 0.0)
    inner = jnp.maximum(smooth - radius, 0.0)
    return (0.25 * outer) * (outer * outer) - inner * (inner * inner)


def prepare_kernel(ints, pos, vel, energy, masses, bins, first, second, near, far, note):
    def measure(cell, totals):
        count = ints[COUNTS + cell]
        chunks = (count + (FORCE_ROWS - 1)) // FORCE_ROWS
        tiles = 1 + (count > 128).astype(I32)
        return totals[0] + chunks, totals[1] + tiles, totals[2] + chunks * tiles

    chunks, tiles, both = lax.fori_loop(0, CELLS, measure, (0, 0, 0), unroll=8)
    for k in range(EXPORT):
        note[k] = ints[COUNTS + ints[EXPORTS + k]]
    note[EXPORT] = chunks
    note[EXPORT + 1] = tiles
    note[EXPORT + 2] = both
    for k in range(EXPORT + 3, 128):
        note[k] = 0

    lane = lax.broadcasted_iota(I32, (1, SLOTS), 1)
    smooth = 0.4 * jnp.exp2(bins[...].astype(F32) * math.log2(1.2))
    made = derived_fields(smooth, energy[...])
    for cell in range(CELLS):
        live = (lane < ints[COUNTS + cell]).astype(F32)
        one = slice(cell, cell + 1)
        for axis in range(3):
            first[cell, axis : axis + 1, :] = pos[axis, one, :]
            first[cell, 5 + axis : 6 + axis, :] = vel[axis, one, :]
        first[cell, 3:4, :] = masses[one, :] * live
        first[cell, 4:5, :] = smooth[one, :]
        for i, value in enumerate(made):
            second[cell, i : i + 1, :] = value[one, :]
        second[cell, 4:5, :] = energy[one, :]
        second[cell, 5:6, :] = live

    def gather(k, carry):
        cell = ints[EXPORTS + k]
        near[k] = first[cell]
        far[k] = second[cell, 4:5, :]
        return carry

    lax.fori_loop(0, EXPORT, gather, 0)


def derived_fields(smooth, energy):
    inverse = pl.reciprocal(smooth, approx=True)
    square = inverse * inverse
    sound = jnp.sqrt(GAMMA_GAS * (GAMMA_GAS - 1.0) * energy) * (1.0 / 40.0)
    return (0.5 * ROOT) * (square * inverse), ROOT * square, sound, 0.05 * smooth


def place_of(side):
    rows, columns = lax.axis_size("gx"), lax.axis_size("yz")
    g = lax.rem(lax.axis_index("gx") + (side // 3 - 1 + rows), rows)
    y = lax.rem(lax.axis_index("yz") + (side % 3 - 1 + columns), columns)
    return g, y


def greet(sides):
    barrier = pltpu.get_barrier_semaphore()
    for side in sides:
        pl.semaphore_signal(barrier, inc=1, device_id=place_of(side), device_id_type=MESH)
    pl.semaphore_wait(barrier, len(sides))


def remote(source, target, send, receive, side):
    return pltpu.make_async_remote_copy(
        src_ref=source,
        dst_ref=target,
        send_sem=send,
        recv_sem=receive,
        device_id=place_of(side),
        device_id_type=MESH,
    )


def part_of(ref, side, piece):
    size = EXPORT // PIECES
    return ref.at[pl.ds(side * EXPORT + piece * size, size)]


def greet_lines():
    barrier = pltpu.get_barrier_semaphore()
    rows, columns = lax.axis_size("gx"), lax.axis_size("yz")
    for step in range(1, rows):
        pl.semaphore_signal(barrier, inc=1, device_id=line_place(step, 0), device_id_type=MESH)
    for step in range(1, columns):
        pl.semaphore_signal(barrier, inc=1, device_id=line_place(0, step), device_id_type=MESH)
    pl.semaphore_wait(barrier, rows + columns - 2)


def line_place(down, over):
    rows, columns = lax.axis_size("gx"), lax.axis_size("yz")
    return lax.rem(lax.axis_index("gx") + down, rows), lax.rem(lax.axis_index("yz") + over, columns)


def gather_lines(every, part, steps, send, receive, place):
    copies = []
    for step in range(1, steps):
        copy = pltpu.make_async_remote_copy(
            src_ref=every.at[part],
            dst_ref=every.at[part],
            send_sem=send.at[step],
            recv_sem=receive.at[step],
            device_id=place(step),
            device_id_type=MESH,
        )
        copy.start()
        copies.append(copy)
    return copies


def halo_kernel(
    near, far, note, near_all, far_all, notes, shares, every, send, receive, row_send, row_receive, column_send, column_receive
):
    columns = lax.axis_size("yz")
    line = lax.axis_index("gx") * columns
    notes[4] = note[0]
    every[line + lax.axis_index("yz")] = note[0]
    greet_lines()
    mine = gather_lines(
        every, pl.ds(line + lax.axis_index("yz"), 1), columns, column_send, column_receive,
        lambda step: line_place(0, step),
    )
    kinds = [(near, near_all, p) for p in range(PIECES)] + [(far, far_all, None), (note, notes, None)]
    started = {}

    def view(ref, slot, piece):
        if piece is not None:
            return part_of(ref, slot, piece)
        size = EXPORT if ref is far_all or ref is far else 1
        return ref.at[pl.ds(slot * size, size)]

    for kind, (own, whole, piece) in enumerate(kinds):
        for side in (7, 1, 5, 3):
            slot = 8 - side
            copy = remote(view(own, 0, piece), view(whole, slot, piece), send.at[kind, slot], receive.at[kind, slot], side)
            copy.start()
            started[kind, slot] = copy
    for copy in mine:
        copy.wait()
    lines = gather_lines(
        every, pl.ds(line, columns), lax.axis_size("gx"), row_send, row_receive,
        lambda step: line_place(step, 0),
    )
    for kind, (own, whole, piece) in enumerate(kinds):
        for came in (1, 7):
            started[kind, came].wait_recv()
            for side in (5, 3):
                slot = came + (-1 if side == 5 else 1)
                copy = remote(view(whole, came, piece), view(whole, slot, piece), send.at[kind, slot], receive.at[kind, slot], side)
                copy.start()
                started[kind, slot] = copy
    for copy in lines:
        copy.wait()
    balance(every, shares)
    for (kind, slot), copy in started.items():
        copy.wait_send()
        if slot not in (1, 7):
            copy.wait_recv()


def swap_all(source, target, send, receive, stride):
    copies = []
    for side in SIDES:
        slot = 8 - side
        piece = source.at[pl.ds(side * EXPORT, EXPORT)] if stride else source
        copy = remote(piece, target.at[pl.ds(slot * EXPORT, EXPORT)], send.at[slot], receive.at[slot], side)
        copy.start()
        copies.append(copy)
    for copy in copies:
        copy.wait()


def total_of(block):
    parts = [block[side * EXPORT : (side + 1) * EXPORT] for side in SIDES]
    return ((parts[0] + parts[1]) + (parts[2] + parts[3])) + ((parts[4] + parts[5]) + (parts[6] + parts[7]))


def combine_kernel(ints, first, second, partial, back, raw, late, late_all, came, sent, total, send, receive):
    greet(SIDES)
    swap_all(back, came, send.at[0], receive.at[0], True)
    total[...] = total_of(came)

    def per_cell(cell, carry):
        slot = ints[SLOT_OF + cell]
        extra = jnp.where(slot >= 0, total[jnp.maximum(slot, 0)], 0.0)
        inverse = pl.reciprocal(first[cell, 4:5, :], approx=True)
        cube = inverse * inverse * inverse
        value = (partial[cell] + extra) * (SIGMA_NORM * cube * cube)
        raw[cell] = value
        rho = jnp.where(second[cell, 5:6, :] > 0, value, 1.0)
        late[cell, 0:1, :] = rho * (1.0 / 200.0)
        late[cell, 1:2, :] = (GAMMA_GAS - 1.0) * second[cell, 4:5, :] * pl.reciprocal(rho, approx=True)
        return carry

    lax.fori_loop(0, CELLS, per_cell, 0)

    def gather(k, carry):
        sent[k] = late[ints[EXPORTS + k], 0:1, :]
        return carry

    lax.fori_loop(0, EXPORT, gather, 0)
    swap_all(sent, late_all, send.at[1], receive.at[1], False)


def return_kernel(back, came, send, receive):
    greet(SIDES)
    swap_all(back, came, send, receive, True)


def balance(every, shares):
    loads = jnp.transpose(every[:, 0, :].astype(F32))
    chunks, tiles, both = (loads[EXPORT + i : EXPORT + i + 1] for i in range(3))
    local = 0.25 * tiles + 0.04 * both + (0.04 / CELLS) * (chunks * tiles)
    lane = lax.broadcasted_iota(I32, (1, 128), 1)
    columns = lax.axis_size("yz")
    place = lax.rem(lane, columns)

    def over(value, step):
        if step == 0:
            return value
        inner = pltpu.roll(value, (128 - step) % 128, 1)
        wrapped = pltpu.roll(value, (step * (columns - 1)) % 128, 1)
        return jnp.where(place == (columns - 1 if step > 0 else 0), wrapped, inner)

    def along(value, up, step):
        moved_up = pltpu.roll(value, (128 - up * columns) % 128, 1) if up else value
        return over(moved_up, step)

    links = [(side // 3 - 1, side % 3 - 1) for side in (5, 6, 7, 8)]
    scale = 0.043 * EXPORT / (CELLS * CELLS)
    costs = [
        (0.5 * scale) * (chunks * along(tiles, *link) + along(chunks, *link) * tiles) for link in links
    ]
    inverse = [0.1 / jnp.maximum(cost, 1e-3) for cost in costs]

    def step(i, parts):
        total = local
        for link, cost, part in zip(links, costs, parts):
            total = total + part * cost + along((1.0 - part) * cost, -link[0], -link[1])
        return tuple(
            jnp.clip(part + (along(total, *link) - total) * inv, 0.0, 1.0)
            for link, inv, part in zip(links, inverse, parts)
        )

    parts = lax.fori_loop(0, 8, step, (jnp.full((1, 128), 0.5, F32),) * 4)
    me = lax.axis_index("gx") * columns + lax.axis_index("yz")
    for i, (link, part) in enumerate(zip(links, parts)):
        count = jnp.floor(part * EXPORT + 0.5)
        for row, value in ((i, count), (4 + i, along(count, -link[0], -link[1]))):
            mine = jnp.sum(jnp.where(lane == me, value, 0.0), axis=1, keepdims=True)
            shares[row : row + 1, :] = jnp.broadcast_to(mine, (1, 128)).astype(I32)


def make_plan(ints, notes, shares, codes, plan):
    def code(j, carry):
        entry = ints[CROSS_LIST + j]
        source, slot = entry & 1023, entry >> 10
        side, place = source >> 5, source & 31
        share = shares[jnp.where(side > 4, side - 5, 7 - side), 0]
        use = jnp.where(side > 4, (place < share).astype(I32), (slot >= share).astype(I32))
        codes[j] = source * 4 + use * (1 + (notes[side, 0, place] > 128).astype(I32))
        return carry

    lax.fori_loop(0, 256, code, 0, unroll=8)

    def put(at, cell):
        plan[at] = 2 * cell
        plan[at + 1] = 2 * cell + 1

    def per_cell(cell, carry):
        local, cross = carry
        plan[LOCAL_FIRST + cell] = local
        plan[CROSS_FIRST + cell] = cross
        count = ints[COUNTS + cell]
        plan[PLAN_COUNTS + cell] = count
        plan[PLAN_SLOTS + cell] = ints[SLOT_OF + cell]
        put(LOCAL_TILES + local, cell)
        local = local + 1 + (count > 128).astype(I32)

        def add_local(j, at):
            target = ints[LOCAL_LIST + j]
            put(LOCAL_TILES + at, target)
            return at + 1 + (ints[COUNTS + target] > 128).astype(I32)

        def add_cross(j, at):
            entry = codes[j]
            put(CROSS_TILES + at, entry >> 2)
            return at + (entry & 3)

        local = lax.fori_loop(ints[LOCAL_STARTS + cell], ints[LOCAL_STARTS + cell + 1], add_local, local)
        cross = lax.fori_loop(ints[CROSS_STARTS + cell], ints[CROSS_STARTS + cell + 1], add_cross, cross)
        return local, cross

    local, cross = lax.fori_loop(0, CELLS, per_cell, (0, 0))
    plan[LOCAL_FIRST + CELLS] = local
    plan[CROSS_FIRST + CELLS] = cross


def density_lanes(held, base, count, table, lanes, add_lane, lane_mass, row_sums):
    size = DENSITY_ROWS
    trips = (count + (size - 1)) // size
    fields = []
    for cell, l in lanes:
        x, y, z, m, h = (table[cell, i : i + 1, l] for i in range(5))
        fields.append((x, y, z, m, h, h + h))

    def chunk(step, totals):
        rows = pl.ds(pl.multiple_of(step * size, size), size)
        rx, ry, rz, mass = (held[base + i, rows, :] for i in range(4))
        if lane_mass:
            rh = held[base + 4, rows, :]
            rh2 = rh + rh
            row_total = row_sums[rows, :]
        result = []
        for total, (x, y, z, m, h1, h2) in zip(totals, fields):
            dx, dy, dz = x - rx, y - ry, z - rz
            dist_sq = jnp.maximum(dx * dx + dy * dy + dz * dz, TINY)
            radius = dist_sq * lax.rsqrt(dist_sq)
            result.append(total + summed_rows(spline_unscaled(radius, h2, h1) * mass))
            if lane_mass:
                row_total = row_total + spline_unscaled(radius, rh2, rh) * m
        if lane_mass:
            row_sums[rows, :] = row_total
        return tuple(result)

    totals = lax.fori_loop(0, trips, chunk, (jnp.zeros((8, 128), F32),) * len(lanes))
    for (cell, l), total in zip(lanes, totals):
        add_lane[cell, :, l] += jnp.sum(total, axis=0, keepdims=True)


def density_kernel(
    ints, notes, shares, table, imports, raw, back, plan, held, sums, codes,
):
    raw[...] = jnp.zeros_like(raw)
    back[...] = jnp.zeros_like(back)
    make_plan(ints, notes, shares, codes, plan)

    def lay(cells, sizes):
        spread([(i, table, i) for i in range(5)], held, cells, sizes, 5)

    def work(cell, place):
        base = place * 5
        count = plan[PLAN_COUNTS + cell]
        slot = plan[PLAN_SLOTS + cell]
        over_part(
            plan, cell, LOCAL_FIRST, LOCAL_TILES,
            lambda lanes: density_lanes(held, base, count, table, lanes, raw, False, None),
        )

        @pl.when(slot >= 0)
        def with_pairs():
            sums[...] = jnp.zeros_like(sums)
            over_part(
                plan, cell, CROSS_FIRST, CROSS_TILES,
                lambda lanes: density_lanes(held, base, count, imports, lanes, back, True, sums),
            )

            def finish(l):
                turned = jnp.transpose(sums[l : l + 128, :])
                raw[cell, :, l : l + 128] += jnp.sum(turned, axis=0, keepdims=True)

            finish(0)

            @pl.when(count > 128)
            def second_half():
                finish(128)

    over_cells(plan, lay, work)


def slope_part(radius, half_beta, beta_h):
    reach = half_beta * radius
    outer = jnp.maximum(beta_h - reach, 0.0)
    least = jnp.minimum(outer, reach)
    return least * (outer + (outer - least))


def force_pair(row, lane):
    dx, dy, dz = lane[0] - row[0], lane[1] - row[1], lane[2] - row[2]
    dist_sq = jnp.maximum(dx * dx + dy * dy + dz * dz, TINY)
    inverse = lax.rsqrt(dist_sq)
    radius = dist_sq * inverse
    slope = (slope_part(radius, row[6], row[7]) + slope_part(radius, lane[6], lane[7])) * inverse
    approach = (lane[3] - row[3]) * dx + (lane[4] - row[4]) * dy + (lane[5] - row[5]) * dz
    smooth = lane[11] + row[11]
    converge = (
        smooth * jnp.minimum(approach, 0.0) * pl.reciprocal(dist_sq + smooth * smooth, approx=True)
    )
    viscous = converge * (converge - (lane[8] + row[8])) * pl.reciprocal(lane[9] + row[9], approx=True)
    lane_term = lane[10] + viscous
    row_term = row[10] + viscous
    return dx, dy, dz, slope, approach, lane_term, row_term


def spread_force(tables, held, cells, counts):
    rows = [(i, tables[t], r) for i, (t, r) in enumerate(FORCE_LANES) if i not in (6, 7, 10, 11)]
    rows.append((13, tables[0], 4))

    def derive(made):
        smooth = made.pop(13)
        inverse = pl.reciprocal(smooth, approx=True)
        square = inverse * inverse
        made[7] = ROOT * square
        made[6] = (0.5 * ROOT) * (square * inverse)
        made[11] = 0.05 * smooth
        made[10] = 4.8 * (made[8] * made[8]) * pl.reciprocal(made[9], approx=True)

    spread(rows, held, cells, counts, 13, derive)


def force_lanes(held, base, count, tables, lanes, add_lane, row_sums, places):
    size = FORCE_ROWS
    trips = (count + (size - 1)) // size
    fields = [[tables[t][cell, i : i + 1, l] for t, i in places] for cell, l in lanes]

    def chunk(step, totals):
        rows = pl.ds(pl.multiple_of(step * size, size), size)
        row = [held[base + i, rows, :] for i in range(13)]
        result = []
        if row_sums is not None:
            row_total = [row_sums[i, rows, :] for i in range(4)]
        for index, lane in enumerate(fields):
            dx, dy, dz, slope, approach, lane_term, row_term = force_pair(row, lane)
            common = lane_term + row_term
            weight = row[12] * slope
            pull = weight * common
            terms = (pull * dx, pull * dy, pull * dz, weight * approach * lane_term)
            result += [t + summed_rows(v) for t, v in zip(totals[4 * index :], terms)]
            if row_sums is not None:
                weight = lane[12] * slope
                pull = weight * common
                terms = (pull * dx, pull * dy, pull * dz, weight * approach * row_term)
                row_total = [t + v for t, v in zip(row_total, terms)]
        if row_sums is not None:
            for i in range(4):
                row_sums[i, rows, :] = row_total[i]
        return tuple(result)

    totals = lax.fori_loop(0, trips, chunk, (jnp.zeros((8, 128), F32),) * (4 * len(lanes)))
    for index, (cell, l) in enumerate(lanes):
        for i in range(4):
            part = jnp.sum(totals[4 * index + i], axis=0, keepdims=True)
            add_lane[cell, i : i + 1, l] += part


def force_kernel(
    plan, first, second, late, imports, energies, densities, own, back, derived, held, row_sums,
):
    own[...] = jnp.zeros_like(own)
    back[...] = jnp.zeros_like(back)
    for side in SIDES:

        def derive(step, carry):
            cells = pl.ds(side * EXPORT + step * 8, 8)
            energy = energies[cells, 0, :]
            rho = densities[cells, 0, :]
            made = derived_fields(imports[cells, 4, :], energy)
            press = (GAMMA_GAS - 1.0) / 200.0 * energy * pl.reciprocal(rho, approx=True)
            for i, value in enumerate(made + (rho, press)):
                derived[cells, i, :] = value
            return carry

        lax.fori_loop(0, EXPORT // 8, derive, 0)
    tables = (first, second, late)
    far_tables = (imports, derived)

    def lay(cells, sizes):
        spread_force(tables, held, cells, sizes)

    def work(cell, place):
        base = place * 13
        count = plan[PLAN_COUNTS + cell]
        slot = plan[PLAN_SLOTS + cell]
        over_part(
            plan, cell, LOCAL_FIRST, LOCAL_TILES,
            lambda lanes: force_lanes(held, base, count, tables, lanes, own, None, FORCE_LANES),
        )

        @pl.when(slot >= 0)
        def with_pairs():
            row_sums[...] = jnp.zeros_like(row_sums)
            over_part(
                plan, cell, CROSS_FIRST, CROSS_TILES,
                lambda lanes: force_lanes(held, base, count, far_tables, lanes, back, row_sums, FORCE_FAR),
            )

            def finish(l):
                for i in range(4):
                    turned = jnp.transpose(row_sums[i, l : l + 128, :])
                    total = jnp.sum(turned, axis=0, keepdims=True)
                    own[cell, i : i + 1, l : l + 128] += total if i == 3 else -total

            finish(0)

            @pl.when(count > 128)
            def second_half():
                finish(128)

    over_cells(plan, lay, work)


def finish_kernel(ints, second, raw, own, came, density, acceleration, rate, extra, total):
    extra[...] = total_of(came)
    total[...] = own[...]

    def add(k, carry):
        total[ints[EXPORTS + k]] += extra[k]
        return carry

    lax.fori_loop(0, EXPORT, add, 0)
    for cell in range(CELLS):
        one = slice(cell, cell + 1)
        live = second[cell, 5:6, :]
        density[one, :] = raw[cell] * live
        for axis in range(3):
            acceleration[axis, one, :] = total[cell, axis : axis + 1, :] * live
        rate[one, :] = -total[cell, 3:4, :] * live


def shape(*dims):
    return jax.ShapeDtypeStruct(dims, F32)


def call(kernel, out, scalars, arrays, scratch, limit=40, collective=None):
    many = isinstance(out, (list, tuple))
    count = len(out) if many else 1
    kinds = [o.dtype for o in out] if many else [out.dtype]
    specs = [
        pl.BlockSpec(memory_space=SMEM if k == I32 and collective is None else VMEM) for k in kinds
    ]
    extra = {} if collective is None else dict(collective_id=collective, has_side_effects=True)
    return pl.pallas_call(
        kernel,
        out_shape=out,
        in_specs=[pl.BlockSpec(memory_space=SMEM)] * len(scalars)
        + [pl.BlockSpec(memory_space=VMEM)] * len(arrays),
        out_specs=specs if many else specs[0],
        scratch_shapes=scratch,
        compiler_params=pltpu.CompilerParams(vmem_limit_bytes=limit << 20, **extra),
    )(*scalars, *arrays)


def grouped(keys, values):
    index = jnp.arange(keys.shape[0], dtype=I32)
    ahead = (keys[None, :] < keys[:, None]) | (
        (keys[None, :] == keys[:, None]) & (index[None, :] < index[:, None])
    )
    place = jnp.sum(ahead.astype(I32), axis=1)
    ordered = jnp.sum(jnp.where(place[None, :] == index[:, None], values[None, :], 0), axis=1)
    cells = jnp.arange(CELLS + 1, dtype=I32)
    starts = jnp.sum((keys[None, :] < cells[:, None]).astype(I32), axis=1)
    return starts, ordered


def body(pos, vel, energy, masses, bins, counts, exports, cross_pairs, local_pairs):
    cell_ids = jnp.arange(CELLS, dtype=I32)
    slots = jnp.arange(EXPORT, dtype=I32)
    is_export = exports[None, :] == cell_ids[:, None]
    slot_of = jnp.sum(jnp.where(is_export, slots[None, :] + 1, 0), axis=1) - 1
    local_starts, local_list = grouped(local_pairs[1], local_pairs[0])
    target_slot = jnp.sum(jnp.where(cross_pairs[0][:, None] == exports[None, :], slots[None, :], 0), axis=1)
    cross_starts, cross_list = grouped(cross_pairs[0], cross_pairs[1] + 1024 * target_slot)
    pad = jnp.zeros((7,), I32)
    ints = jnp.concatenate(
        [counts, slot_of, exports, local_starts, pad, local_list, cross_starts, pad, cross_list]
    )
    sems = pltpu.SemaphoreType.DMA
    first, second, near, far, note = call(
        prepare_kernel,
        [shape(CELLS, 8, SLOTS), shape(CELLS, 8, SLOTS), shape(EXPORT, 8, SLOTS), shape(EXPORT, 1, SLOTS),
         jax.ShapeDtypeStruct((128,), I32)],
        [ints],
        [pos, vel, energy, masses, bins],
        [],
        60,
    )
    imports, energies, notes, shares = call(
        halo_kernel,
        [
            shape(9 * EXPORT, 8, SLOTS),
            shape(9 * EXPORT, 1, SLOTS),
            jax.ShapeDtypeStruct((9, 1, 128), I32),
            jax.ShapeDtypeStruct((8, 128), I32),
        ],
        [],
        [near, far, note[None, None]],
        [VMEM((128, 1, 128), I32)] + [sems(d) for d in ((PIECES + 2, 9),) * 2 + ((16,),) * 2 + ((8,),) * 2],
        40,
        0,
    )
    partial, back, plan = call(
        density_kernel,
        [shape(CELLS, 1, SLOTS), shape(9 * EXPORT, 1, SLOTS), jax.ShapeDtypeStruct((PLAN_SIZE,), I32)],
        [ints, notes, shares],
        [first, imports],
        [VMEM((5 * TOGETHER, SLOTS, 128), F32), VMEM((SLOTS, 128), F32), SMEM((256,), I32)],
    )
    raw, late, densities = call(
        combine_kernel,
        [shape(CELLS, 1, SLOTS), shape(CELLS, 2, SLOTS), shape(9 * EXPORT, 1, SLOTS)],
        [ints],
        [first, second, partial, back],
        [
            VMEM((9 * EXPORT, 1, SLOTS), F32),
            VMEM((EXPORT, 1, SLOTS), F32),
            VMEM((EXPORT, 1, SLOTS), F32),
            sems((2, 9)),
            sems((2, 9)),
        ],
        40,
        1,
    )
    own, back = call(
        force_kernel,
        [shape(CELLS, 4, SLOTS), shape(9 * EXPORT, 4, SLOTS)],
        [plan],
        [first, second, late, imports, energies, densities],
        [
            VMEM((9 * EXPORT, 8, SLOTS), F32),
            VMEM((13 * TOGETHER, SLOTS, 128), F32),
            VMEM((4, SLOTS, 128), F32),
        ],
    )
    came = call(
        return_kernel,
        shape(9 * EXPORT, 4, SLOTS),
        [],
        [back],
        [sems((9,)), sems((9,))],
        40,
        2,
    )
    return tuple(
        call(
            finish_kernel,
            [shape(CELLS, SLOTS), shape(3, CELLS, SLOTS), shape(CELLS, SLOTS)],
            [ints],
            [second, raw, own, came],
            [VMEM((EXPORT, 4, SLOTS), F32), VMEM((CELLS, 4, SLOTS), F32)],
        )
    )


def solution(mesh):
    both = ("gx", "yz")
    return jax.shard_map(
        body,
        mesh=mesh,
        in_specs=(
            P(None, both, None),
            P(None, both, None),
            P(both, None),
            P(both, None),
            P(both, None),
            P(both),
            P(both),
            P(None, both),
            P(None, both),
        ),
        out_specs=(P(both, None), P(None, both, None), P(both, None)),
        check_vma=False,
    )
```

```python
import math

import jax
import jax.numpy as jnp
from jax import lax
from jax.experimental import pallas as pl
from jax.experimental.pallas import tpu as pltpu
from jax.sharding import PartitionSpec as P

F32, I32 = jnp.float32, jnp.int32
SIGMA_NORM = 0.3183098861837907
GAMMA_GAS = 5.0 / 3.0
TINY = 1e-24
CELLS, SLOTS, EXPORT = 64, 256, 32
PIECES = 4
TOGETHER = 8
COUNTS, SLOT_OF, EXPORTS, LOCAL_STARTS, LOCAL_LIST, CROSS_STARTS, CROSS_LIST = 0, 64, 128, 160, 232, 296, 368
LOCAL_FIRST, CROSS_FIRST, PLAN_COUNTS, PLAN_SLOTS, LOCAL_TILES, CROSS_TILES, PLAN_SIZE = 0, 72, 144, 208, 272, 536, 1088
DENSITY_ROWS = 32
FORCE_ROWS = 32
ROOT = math.sqrt(1.5 * SIGMA_NORM)
VMEM, SMEM = pltpu.VMEM, pltpu.SMEM
MESH = pl.DeviceIdType.MESH
DENSITY_PICKED, DENSITY_TURNED = (0, 1, 2, 3), (4,)
FORCE_PICKED = (0, 1, 2, 3, 4, 5, 12)
SIDES = (0, 1, 2, 3, 5, 6, 7, 8)
FORCE_LANES = [(0, 0), (0, 1), (0, 2), (0, 5), (0, 6), (0, 7), (1, 0), (1, 1), (1, 2), (2, 0), (2, 1), (1, 3), (0, 3)]
FORCE_FAR = [(0, 0), (0, 1), (0, 2), (0, 5), (0, 6), (0, 7), (1, 0), (1, 1), (1, 2), (1, 4), (1, 5), (1, 3), (0, 3)]


def over_tiles(plan, start, count, block):
    def tile(index):
        entry = plan[start + index]
        return entry // 2, pl.ds(pl.multiple_of((entry % 2) * 128, 128), 128)

    def two(step, carry):
        block((tile(2 * step), tile(2 * step + 1)))
        return carry

    lax.fori_loop(0, count // 2, two, 0)

    @pl.when(count % 2 == 1)
    def last():
        block((tile(count - 1),))


def over_part(plan, cell, firsts, tiles, block):
    start = plan[firsts + cell]
    over_tiles(plan, tiles + start, plan[firsts + cell + 1] - start, block)


def flipped(row):
    return jnp.transpose(jnp.broadcast_to(row, (128, 128)))


def split(values):
    high = values.astype(jnp.bfloat16)
    rest = values - high.astype(F32)
    middle = rest.astype(jnp.bfloat16)
    return high, middle, (rest - middle.astype(F32)).astype(jnp.bfloat16)


def picker(rows):
    width = 128 * len(rows)
    part = lax.rem(lax.broadcasted_iota(I32, (32, width), 0), 8)
    inside = lax.broadcasted_iota(I32, (32, width), 0) < 24
    block = lax.broadcasted_iota(I32, (32, width), 1) // 128
    wanted = jnp.zeros((32, width), I32)
    for i, row in enumerate(rows):
        wanted = jnp.where(block == i, row, wanted)
    return jnp.where(inside & (part == wanted), 1.0, 0.0).astype(jnp.bfloat16)


def spread(rows, target, cells, counts, size, table8, picked, pick, derive=None):
    def half(place, cell, start):
        made = {}
        parts = split(table8[cell, :, start : start + 128])
        left = jnp.concatenate(parts + (jnp.zeros((8, 128), jnp.bfloat16),), axis=0)
        spreads = lax.dot_general(
            left, pick[...], (((0,), (0,)), ((), ())), preferred_element_type=F32
        )
        for i, slot in enumerate(picked):
            made[slot] = spreads[:, 128 * i : 128 * i + 128]
        for slot, table, row in rows:
            made[slot] = flipped(table[cell, row : row + 1, start : start + 128])
        if derive is not None:
            derive(made)
        for slot, value in made.items():
            target[place * size + slot, start : start + 128, :] = value

    for place, cell in enumerate(cells):
        half(place, cell, 0)
    for place, cell in enumerate(cells):

        @pl.when(counts[place] > 128)
        def second_half():
            half(place, cell, 128)


def over_cells(plan, lay, work):
    def group(step, carry):
        cells = [step * TOGETHER + i for i in range(TOGETHER)]
        lay(cells, [plan[PLAN_COUNTS + cell] for cell in cells])
        lax.fori_loop(0, TOGETHER, lambda i, c: (work(step * TOGETHER + i, i), c)[1], 0)
        return carry

    lax.fori_loop(0, CELLS // TOGETHER, group, 0)


def summed_rows(values):
    return jnp.sum(values.reshape(values.shape[0] // 8, 8, 128), axis=0)


def spline_unscaled(radius, smooth_twice, smooth):
    outer = jnp.maximum(smooth_twice - radius, 0.0)
    inner = jnp.maximum(smooth - radius, 0.0)
    return (0.25 * outer) * (outer * outer) - inner * (inner * inner)


def prepare_kernel(ints, pos, vel, energy, masses, bins, first, second, near, far, note):
    def measure(cell, totals):
        count = ints[COUNTS + cell]
        chunks = (count + (FORCE_ROWS - 1)) // FORCE_ROWS
        tiles = 1 + (count > 128).astype(I32)
        return totals[0] + chunks, totals[1] + tiles, totals[2] + chunks * tiles

    chunks, tiles, both = lax.fori_loop(0, CELLS, measure, (0, 0, 0), unroll=8)
    for k in range(EXPORT):
        note[k] = ints[COUNTS + ints[EXPORTS + k]]
    note[EXPORT] = chunks
    note[EXPORT + 1] = tiles
    note[EXPORT + 2] = both
    for k in range(EXPORT + 3, 128):
        note[k] = 0

    lane = lax.broadcasted_iota(I32, (1, SLOTS), 1)
    smooth = 0.4 * jnp.exp2(bins[...].astype(F32) * math.log2(1.2))
    made = derived_fields(smooth, energy[...])
    for cell in range(CELLS):
        live = (lane < ints[COUNTS + cell]).astype(F32)
        one = slice(cell, cell + 1)
        for axis in range(3):
            first[cell, axis : axis + 1, :] = pos[axis, one, :]
            first[cell, 5 + axis : 6 + axis, :] = vel[axis, one, :]
        first[cell, 3:4, :] = masses[one, :] * live
        first[cell, 4:5, :] = smooth[one, :]
        for i, value in enumerate(made):
            second[cell, i : i + 1, :] = value[one, :]
        second[cell, 4:5, :] = energy[one, :]
        second[cell, 5:6, :] = live

    def gather(k, carry):
        cell = ints[EXPORTS + k]
        near[k] = first[cell]
        far[k] = second[cell, 4:5, :]
        return carry

    lax.fori_loop(0, EXPORT, gather, 0, unroll=8)


def derived_fields(smooth, energy):
    inverse = pl.reciprocal(smooth, approx=True)
    square = inverse * inverse
    sound = jnp.sqrt(GAMMA_GAS * (GAMMA_GAS - 1.0) * energy) * (1.0 / 40.0)
    return (0.5 * ROOT) * (square * inverse), ROOT * square, sound, 0.05 * smooth


def place_of(side):
    rows, columns = lax.axis_size("gx"), lax.axis_size("yz")
    g = lax.rem(lax.axis_index("gx") + (side // 3 - 1 + rows), rows)
    y = lax.rem(lax.axis_index("yz") + (side % 3 - 1 + columns), columns)
    return g, y


def greet(sides):
    barrier = pltpu.get_barrier_semaphore()
    for side in sides:
        pl.semaphore_signal(barrier, inc=1, device_id=place_of(side), device_id_type=MESH)
    pl.semaphore_wait(barrier, len(sides))


def remote(source, target, send, receive, side):
    return pltpu.make_async_remote_copy(
        src_ref=source,
        dst_ref=target,
        send_sem=send,
        recv_sem=receive,
        device_id=place_of(side),
        device_id_type=MESH,
    )


def part_of(ref, side, piece):
    size = EXPORT // PIECES
    return ref.at[pl.ds(side * EXPORT + piece * size, size)]


def greet_lines():
    barrier = pltpu.get_barrier_semaphore()
    rows, columns = lax.axis_size("gx"), lax.axis_size("yz")
    for step in range(1, rows):
        pl.semaphore_signal(barrier, inc=1, device_id=line_place(step, 0), device_id_type=MESH)
    for step in range(1, columns):
        pl.semaphore_signal(barrier, inc=1, device_id=line_place(0, step), device_id_type=MESH)
    pl.semaphore_wait(barrier, rows + columns - 2)


def line_place(down, over):
    rows, columns = lax.axis_size("gx"), lax.axis_size("yz")
    return lax.rem(lax.axis_index("gx") + down, rows), lax.rem(lax.axis_index("yz") + over, columns)


def gather_lines(every, part, steps, send, receive, place):
    copies = []
    for step in range(1, steps):
        copy = pltpu.make_async_remote_copy(
            src_ref=every.at[part],
            dst_ref=every.at[part],
            send_sem=send.at[step],
            recv_sem=receive.at[step],
            device_id=place(step),
            device_id_type=MESH,
        )
        copy.start()
        copies.append(copy)
    return copies


def halo_kernel(
    near, far, note, near_all, far_all, notes, shares, every, send, receive, row_send, row_receive, column_send, column_receive
):
    columns = lax.axis_size("yz")
    line = lax.axis_index("gx") * columns
    notes[4] = note[0]
    every[line + lax.axis_index("yz")] = note[0]
    greet_lines()
    mine = gather_lines(
        every, pl.ds(line + lax.axis_index("yz"), 1), columns, column_send, column_receive,
        lambda step: line_place(0, step),
    )
    kinds = [(near, near_all, p) for p in range(PIECES)] + [(far, far_all, None), (note, notes, None)]
    started = {}

    def view(ref, slot, piece):
        if piece is not None:
            return part_of(ref, slot, piece)
        size = EXPORT if ref is far_all or ref is far else 1
        return ref.at[pl.ds(slot * size, size)]

    for kind, (own, whole, piece) in enumerate(kinds):
        for side in (7, 1, 5, 3):
            slot = 8 - side
            copy = remote(view(own, 0, piece), view(whole, slot, piece), send.at[kind, slot], receive.at[kind, slot], side)
            copy.start()
            started[kind, slot] = copy
    for copy in mine:
        copy.wait()
    lines = gather_lines(
        every, pl.ds(line, columns), lax.axis_size("gx"), row_send, row_receive,
        lambda step: line_place(step, 0),
    )
    for kind, (own, whole, piece) in enumerate(kinds):
        for came in (1, 7):
            started[kind, came].wait_recv()
            for side in (5, 3):
                slot = came + (-1 if side == 5 else 1)
                copy = remote(view(whole, came, piece), view(whole, slot, piece), send.at[kind, slot], receive.at[kind, slot], side)
                copy.start()
                started[kind, slot] = copy
    for copy in lines:
        copy.wait()
    balance(every, shares)
    for (kind, slot), copy in started.items():
        copy.wait_send()
        if slot not in (1, 7):
            copy.wait_recv()


def swap_all(source, target, send, receive, stride):
    copies = []
    for side in SIDES:
        slot = 8 - side
        piece = source.at[pl.ds(side * EXPORT, EXPORT)] if stride else source
        copy = remote(piece, target.at[pl.ds(slot * EXPORT, EXPORT)], send.at[slot], receive.at[slot], side)
        copy.start()
        copies.append(copy)
    for copy in copies:
        copy.wait()


def total_of(block):
    parts = [block[side * EXPORT : (side + 1) * EXPORT] for side in SIDES]
    return ((parts[0] + parts[1]) + (parts[2] + parts[3])) + ((parts[4] + parts[5]) + (parts[6] + parts[7]))


def combine_kernel(ints, first, second, partial, back, raw, late, late_all, came, sent, total, send, receive):
    greet(SIDES)
    swap_all(back, came, send.at[0], receive.at[0], True)
    total[...] = total_of(came)

    def per_cell(cell, carry):
        slot = ints[SLOT_OF + cell]
        extra = jnp.where(slot >= 0, total[jnp.maximum(slot, 0)], 0.0)
        inverse = pl.reciprocal(first[cell, 4:5, :], approx=True)
        cube = inverse * inverse * inverse
        value = (partial[cell] + extra) * (SIGMA_NORM * cube * cube)
        raw[cell] = value
        rho = jnp.where(second[cell, 5:6, :] > 0, value, 1.0)
        late[cell, 0:1, :] = rho * (1.0 / 200.0)
        late[cell, 1:2, :] = (GAMMA_GAS - 1.0) * second[cell, 4:5, :] * pl.reciprocal(rho, approx=True)
        return carry

    lax.fori_loop(0, CELLS, per_cell, 0, unroll=8)

    def gather(k, carry):
        sent[k] = late[ints[EXPORTS + k], 0:1, :]
        return carry

    lax.fori_loop(0, EXPORT, gather, 0, unroll=8)
    swap_all(sent, late_all, send.at[1], receive.at[1], False)


def return_kernel(back, came, send, receive):
    greet(SIDES)
    swap_all(back, came, send, receive, True)


def balance(every, shares):
    loads = jnp.transpose(every[:, 0, :].astype(F32))
    chunks, tiles, both = (loads[EXPORT + i : EXPORT + i + 1] for i in range(3))
    local = 0.25 * tiles + 0.04 * both + (0.04 / CELLS) * (chunks * tiles)
    lane = lax.broadcasted_iota(I32, (1, 128), 1)
    columns = lax.axis_size("yz")
    place = lax.rem(lane, columns)

    def over(value, step):
        if step == 0:
            return value
        inner = pltpu.roll(value, (128 - step) % 128, 1)
        wrapped = pltpu.roll(value, (step * (columns - 1)) % 128, 1)
        return jnp.where(place == (columns - 1 if step > 0 else 0), wrapped, inner)

    def along(value, up, step):
        moved_up = pltpu.roll(value, (128 - up * columns) % 128, 1) if up else value
        return over(moved_up, step)

    links = [(side // 3 - 1, side % 3 - 1) for side in (5, 6, 7, 8)]
    scale = 0.043 * EXPORT / (CELLS * CELLS)
    costs = [
        (0.5 * scale) * (chunks * along(tiles, *link) + along(chunks, *link) * tiles) for link in links
    ]
    inverse = [0.1 / jnp.maximum(cost, 1e-3) for cost in costs]

    def step(i, parts):
        total = local
        for link, cost, part in zip(links, costs, parts):
            total = total + part * cost + along((1.0 - part) * cost, -link[0], -link[1])
        return tuple(
            jnp.clip(part + (along(total, *link) - total) * inv, 0.0, 1.0)
            for link, inv, part in zip(links, inverse, parts)
        )

    parts = lax.fori_loop(0, 8, step, (jnp.full((1, 128), 0.5, F32),) * 4)
    me = lax.axis_index("gx") * columns + lax.axis_index("yz")
    for i, (link, part) in enumerate(zip(links, parts)):
        count = jnp.floor(part * EXPORT + 0.5)
        for row, value in ((i, count), (4 + i, along(count, -link[0], -link[1]))):
            mine = jnp.sum(jnp.where(lane == me, value, 0.0), axis=1, keepdims=True)
            shares[row : row + 1, :] = jnp.broadcast_to(mine, (1, 128)).astype(I32)


def make_plan(ints, notes, shares, codes, plan):
    def code(j, carry):
        entry = ints[CROSS_LIST + j]
        source, slot = entry & 1023, ints[SLOT_OF + (entry >> 10)]
        side, place = source >> 5, source & 31
        share = shares[jnp.where(side > 4, side - 5, 7 - side), 0]
        use = jnp.where(side > 4, (place < share).astype(I32), (slot >= share).astype(I32))
        codes[j] = source * 4 + use * (1 + (notes[side, 0, place] > 128).astype(I32))
        return carry

    lax.fori_loop(0, 256, code, 0, unroll=8)

    def put(at, cell):
        plan[at] = 2 * cell
        plan[at + 1] = 2 * cell + 1

    def per_cell(cell, carry):
        local, cross = carry
        plan[LOCAL_FIRST + cell] = local
        plan[CROSS_FIRST + cell] = cross
        count = ints[COUNTS + cell]
        plan[PLAN_COUNTS + cell] = count
        plan[PLAN_SLOTS + cell] = ints[SLOT_OF + cell]
        put(LOCAL_TILES + local, cell)
        local = local + 1 + (count > 128).astype(I32)

        def add_local(j, at):
            target = ints[LOCAL_LIST + j]
            put(LOCAL_TILES + at, target)
            return at + 1 + (ints[COUNTS + target] > 128).astype(I32)

        def add_cross(j, at):
            entry = codes[j]
            put(CROSS_TILES + at, entry >> 2)
            return at + (entry & 3)

        local = lax.fori_loop(ints[LOCAL_STARTS + cell], ints[LOCAL_STARTS + cell + 1], add_local, local)
        cross = lax.fori_loop(ints[CROSS_STARTS + cell], ints[CROSS_STARTS + cell + 1], add_cross, cross)
        return local, cross

    local, cross = lax.fori_loop(0, CELLS, per_cell, (0, 0))
    plan[LOCAL_FIRST + CELLS] = local
    plan[CROSS_FIRST + CELLS] = cross


def density_lanes(held, base, count, table, lanes, add_lane, lane_mass, row_sums):
    size = DENSITY_ROWS
    trips = (count + (size - 1)) // size
    fields = []
    for cell, l in lanes:
        x, y, z, m, h = (table[cell, i : i + 1, l] for i in range(5))
        fields.append((x, y, z, m, h, h + h))

    def chunk(step, totals):
        rows = pl.ds(pl.multiple_of(step * size, size), size)
        rx, ry, rz, mass = (held[base + i, rows, :] for i in range(4))
        if lane_mass:
            rh = held[base + 4, rows, :]
            rh2 = rh + rh
            row_total = row_sums[rows, :]
        result = []
        for total, (x, y, z, m, h1, h2) in zip(totals, fields):
            dx, dy, dz = x - rx, y - ry, z - rz
            dist_sq = jnp.maximum(dx * dx + dy * dy + dz * dz, TINY)
            radius = dist_sq * lax.rsqrt(dist_sq)
            result.append(total + summed_rows(spline_unscaled(radius, h2, h1) * mass))
            if lane_mass:
                row_total = row_total + spline_unscaled(radius, rh2, rh) * m
        if lane_mass:
            row_sums[rows, :] = row_total
        return tuple(result)

    totals = lax.fori_loop(0, trips, chunk, (jnp.zeros((8, 128), F32),) * len(lanes))
    for (cell, l), total in zip(lanes, totals):
        add_lane[cell, :, l] += jnp.sum(total, axis=0, keepdims=True)


def density_kernel(
    ints, notes, shares, table, imports, raw, back, plan, held, sums, codes, pick,
):
    raw[...] = jnp.zeros_like(raw)
    back[...] = jnp.zeros_like(back)
    make_plan(ints, notes, shares, codes, plan)
    pick[...] = picker(DENSITY_PICKED)

    def lay(cells, sizes):
        spread([(i, table, i) for i in DENSITY_TURNED], held, cells, sizes, 5, table, DENSITY_PICKED, pick)

    def work(cell, place):
        base = place * 5
        count = plan[PLAN_COUNTS + cell]
        slot = plan[PLAN_SLOTS + cell]
        over_part(
            plan, cell, LOCAL_FIRST, LOCAL_TILES,
            lambda lanes: density_lanes(held, base, count, table, lanes, raw, False, None),
        )

        @pl.when(slot >= 0)
        def with_pairs():
            sums[...] = jnp.zeros_like(sums)
            over_part(
                plan, cell, CROSS_FIRST, CROSS_TILES,
                lambda lanes: density_lanes(held, base, count, imports, lanes, back, True, sums),
            )

            def finish(l):
                turned = jnp.transpose(sums[l : l + 128, :])
                raw[cell, :, l : l + 128] += jnp.sum(turned, axis=0, keepdims=True)

            finish(0)

            @pl.when(count > 128)
            def second_half():
                finish(128)

    over_cells(plan, lay, work)


def slope_part(radius, half_beta, beta_h):
    reach = half_beta * radius
    outer = jnp.maximum(beta_h - reach, 0.0)
    least = jnp.minimum(outer, reach)
    return least * (outer + (outer - least))


def force_pair(row, lane):
    dx, dy, dz = lane[0] - row[0], lane[1] - row[1], lane[2] - row[2]
    dist_sq = jnp.maximum(dx * dx + dy * dy + dz * dz, TINY)
    inverse = lax.rsqrt(dist_sq)
    radius = dist_sq * inverse
    slope = (slope_part(radius, row[6], row[7]) + slope_part(radius, lane[6], lane[7])) * inverse
    approach = (lane[3] - row[3]) * dx + (lane[4] - row[4]) * dy + (lane[5] - row[5]) * dz
    smooth = lane[11] + row[11]
    converge = (
        smooth * jnp.minimum(approach, 0.0) * pl.reciprocal(dist_sq + smooth * smooth, approx=True)
    )
    viscous = converge * (converge - (lane[8] + row[8])) * pl.reciprocal(lane[9] + row[9], approx=True)
    lane_term = lane[10] + viscous
    row_term = row[10] + viscous
    return dx, dy, dz, slope, approach, lane_term, row_term


def spread_force(tables, held, cells, counts, pick):
    rows = [(i, tables[t], r) for i, (t, r) in enumerate(FORCE_LANES) if i not in (6, 7, 10, 11) + FORCE_PICKED]
    rows.append((13, tables[0], 4))

    def derive(made):
        smooth = made.pop(13)
        inverse = pl.reciprocal(smooth, approx=True)
        square = inverse * inverse
        made[7] = ROOT * square
        made[6] = (0.5 * ROOT) * (square * inverse)
        made[11] = 0.05 * smooth
        made[10] = 4.8 * (made[8] * made[8]) * pl.reciprocal(made[9], approx=True)

    spread(rows, held, cells, counts, 13, tables[0], FORCE_PICKED, pick, derive)


def force_lanes(held, base, count, tables, lanes, add_lane, row_sums, places):
    size = FORCE_ROWS
    trips = (count + (size - 1)) // size
    fields = [[tables[t][cell, i : i + 1, l] for t, i in places] for cell, l in lanes]

    def chunk(step, totals):
        rows = pl.ds(pl.multiple_of(step * size, size), size)
        row = [held[base + i, rows, :] for i in range(13)]
        result = []
        if row_sums is not None:
            row_total = [row_sums[i, rows, :] for i in range(4)]
        for index, lane in enumerate(fields):
            dx, dy, dz, slope, approach, lane_term, row_term = force_pair(row, lane)
            common = lane_term + row_term
            weight = row[12] * slope
            pull = weight * common
            terms = (pull * dx, pull * dy, pull * dz, weight * approach * lane_term)
            result += [t + summed_rows(v) for t, v in zip(totals[4 * index :], terms)]
            if row_sums is not None:
                weight = lane[12] * slope
                pull = weight * common
                terms = (pull * dx, pull * dy, pull * dz, weight * approach * row_term)
                row_total = [t + v for t, v in zip(row_total, terms)]
        if row_sums is not None:
            for i in range(4):
                row_sums[i, rows, :] = row_total[i]
        return tuple(result)

    totals = lax.fori_loop(0, trips, chunk, (jnp.zeros((8, 128), F32),) * (4 * len(lanes)))
    for index, (cell, l) in enumerate(lanes):
        for i in range(4):
            part = jnp.sum(totals[4 * index + i], axis=0, keepdims=True)
            add_lane[cell, i : i + 1, l] += part


def force_kernel(
    plan, first, second, late, imports, energies, densities, own, back, derived, held, row_sums, pick,
):
    own[...] = jnp.zeros_like(own)
    back[...] = jnp.zeros_like(back)
    for side in SIDES:

        def derive(step, carry):
            cells = pl.ds(side * EXPORT + step * 8, 8)
            energy = energies[cells, 0, :]
            rho = densities[cells, 0, :]
            made = derived_fields(imports[cells, 4, :], energy)
            press = (GAMMA_GAS - 1.0) / 200.0 * energy * pl.reciprocal(rho, approx=True)
            for i, value in enumerate(made + (rho, press)):
                derived[cells, i, :] = value
            return carry

        lax.fori_loop(0, EXPORT // 8, derive, 0)
    pick[...] = picker([FORCE_LANES[i][1] for i in FORCE_PICKED])
    tables = (first, second, late)
    far_tables = (imports, derived)

    def lay(cells, sizes):
        spread_force(tables, held, cells, sizes, pick)

    def work(cell, place):
        base = place * 13
        count = plan[PLAN_COUNTS + cell]
        slot = plan[PLAN_SLOTS + cell]
        over_part(
            plan, cell, LOCAL_FIRST, LOCAL_TILES,
            lambda lanes: force_lanes(held, base, count, tables, lanes, own, None, FORCE_LANES),
        )

        @pl.when(slot >= 0)
        def with_pairs():
            row_sums[...] = jnp.zeros_like(row_sums)
            over_part(
                plan, cell, CROSS_FIRST, CROSS_TILES,
                lambda lanes: force_lanes(held, base, count, far_tables, lanes, back, row_sums, FORCE_FAR),
            )

            def finish(l):
                for i in range(4):
                    turned = jnp.transpose(row_sums[i, l : l + 128, :])
                    total = jnp.sum(turned, axis=0, keepdims=True)
                    own[cell, i : i + 1, l : l + 128] += total if i == 3 else -total

            finish(0)

            @pl.when(count > 128)
            def second_half():
                finish(128)

    over_cells(plan, lay, work)


def finish_kernel(ints, second, raw, own, came, density, acceleration, rate, extra, total):
    extra[...] = total_of(came)
    total[...] = own[...]

    def add(k, carry):
        total[ints[EXPORTS + k]] += extra[k]
        return carry

    lax.fori_loop(0, EXPORT, add, 0, unroll=4)
    for cell in range(CELLS):
        one = slice(cell, cell + 1)
        live = second[cell, 5:6, :]
        density[one, :] = raw[cell] * live
        for axis in range(3):
            acceleration[axis, one, :] = total[cell, axis : axis + 1, :] * live
        rate[one, :] = -total[cell, 3:4, :] * live


def shape(*dims):
    return jax.ShapeDtypeStruct(dims, F32)


def call(kernel, out, scalars, arrays, scratch, limit=40, collective=None):
    many = isinstance(out, (list, tuple))
    count = len(out) if many else 1
    kinds = [o.dtype for o in out] if many else [out.dtype]
    specs = [
        pl.BlockSpec(memory_space=SMEM if k == I32 and collective is None else VMEM) for k in kinds
    ]
    extra = {} if collective is None else dict(collective_id=collective, has_side_effects=True)
    return pl.pallas_call(
        kernel,
        out_shape=out,
        in_specs=[pl.BlockSpec(memory_space=SMEM)] * len(scalars)
        + [pl.BlockSpec(memory_space=VMEM)] * len(arrays),
        out_specs=specs if many else specs[0],
        scratch_shapes=scratch,
        compiler_params=pltpu.CompilerParams(vmem_limit_bytes=limit << 20, **extra),
    )(*scalars, *arrays)


def grouped(keys, values):
    index = jnp.arange(keys.shape[0], dtype=I32)
    ahead = (keys[None, :] < keys[:, None]) | (
        (keys[None, :] == keys[:, None]) & (index[None, :] < index[:, None])
    )
    place = jnp.sum(ahead.astype(I32), axis=1)
    ordered = jnp.sum(jnp.where(place[None, :] == index[:, None], values[None, :], 0), axis=1)
    cells = jnp.arange(CELLS + 1, dtype=I32)
    starts = jnp.sum((keys[None, :] < cells[:, None]).astype(I32), axis=1)
    return starts, ordered


def body(pos, vel, energy, masses, bins, counts, exports, cross_pairs, local_pairs):
    cell_ids = jnp.arange(CELLS, dtype=I32)
    slots = jnp.arange(EXPORT, dtype=I32)
    is_export = exports[None, :] == cell_ids[:, None]
    slot_of = jnp.sum(jnp.where(is_export, slots[None, :] + 1, 0), axis=1) - 1
    local_starts, local_list = grouped(local_pairs[1], local_pairs[0])
    cross_starts, cross_list = grouped(cross_pairs[0], cross_pairs[1] + 1024 * cross_pairs[0])
    pad = jnp.zeros((7,), I32)
    ints = jnp.concatenate(
        [counts, slot_of, exports, local_starts, pad, local_list, cross_starts, pad, cross_list]
    )
    sems = pltpu.SemaphoreType.DMA
    first, second, near, far, note = call(
        prepare_kernel,
        [shape(CELLS, 8, SLOTS), shape(CELLS, 8, SLOTS), shape(EXPORT, 8, SLOTS), shape(EXPORT, 1, SLOTS),
         jax.ShapeDtypeStruct((128,), I32)],
        [ints],
        [pos, vel, energy, masses, bins],
        [],
        60,
    )
    imports, energies, notes, shares = call(
        halo_kernel,
        [
            shape(9 * EXPORT, 8, SLOTS),
            shape(9 * EXPORT, 1, SLOTS),
            jax.ShapeDtypeStruct((9, 1, 128), I32),
            jax.ShapeDtypeStruct((8, 128), I32),
        ],
        [],
        [near, far, note[None, None]],
        [VMEM((128, 1, 128), I32)] + [sems(d) for d in ((PIECES + 2, 9),) * 2 + ((16,),) * 2 + ((8,),) * 2],
        40,
        0,
    )
    partial, back, plan = call(
        density_kernel,
        [shape(CELLS, 1, SLOTS), shape(9 * EXPORT, 1, SLOTS), jax.ShapeDtypeStruct((PLAN_SIZE,), I32)],
        [ints, notes, shares],
        [first, imports],
        [VMEM((5 * TOGETHER, SLOTS, 128), F32), VMEM((SLOTS, 128), F32), SMEM((256,), I32),
         VMEM((32, 128 * len(DENSITY_PICKED)), jnp.bfloat16)],
    )
    raw, late, densities = call(
        combine_kernel,
        [shape(CELLS, 1, SLOTS), shape(CELLS, 2, SLOTS), shape(9 * EXPORT, 1, SLOTS)],
        [ints],
        [first, second, partial, back],
        [
            VMEM((9 * EXPORT, 1, SLOTS), F32),
            VMEM((EXPORT, 1, SLOTS), F32),
            VMEM((EXPORT, 1, SLOTS), F32),
            sems((2, 9)),
            sems((2, 9)),
        ],
        40,
        1,
    )
    own, back = call(
        force_kernel,
        [shape(CELLS, 4, SLOTS), shape(9 * EXPORT, 4, SLOTS)],
        [plan],
        [first, second, late, imports, energies, densities],
        [
            VMEM((9 * EXPORT, 8, SLOTS), F32),
            VMEM((13 * TOGETHER, SLOTS, 128), F32),
            VMEM((4, SLOTS, 128), F32),
            VMEM((32, 128 * len(FORCE_PICKED)), jnp.bfloat16),
        ],
    )
    came = call(
        return_kernel,
        shape(9 * EXPORT, 4, SLOTS),
        [],
        [back],
        [sems((9,)), sems((9,))],
        40,
        2,
    )
    return tuple(
        call(
            finish_kernel,
            [shape(CELLS, SLOTS), shape(3, CELLS, SLOTS), shape(CELLS, SLOTS)],
            [ints],
            [second, raw, own, came],
            [VMEM((EXPORT, 4, SLOTS), F32), VMEM((CELLS, 4, SLOTS), F32)],
        )
    )


def solution(mesh):
    both = ("gx", "yz")
    return jax.shard_map(
        body,
        mesh=mesh,
        in_specs=(
            P(None, both, None),
            P(None, both, None),
            P(both, None),
            P(both, None),
            P(both, None),
            P(both),
            P(both),
            P(None, both),
            P(None, both),
        ),
        out_specs=(P(both, None), P(None, both, None), P(both, None)),
        check_vma=False,
    )
```

```python
import math

import jax
import jax.numpy as jnp
from jax import lax
from jax.experimental import pallas as pl
from jax.experimental.pallas import tpu as pltpu
from jax.sharding import PartitionSpec as P

F32, I32 = jnp.float32, jnp.int32
SIGMA_NORM = 0.3183098861837907
GAMMA_GAS = 5.0 / 3.0
TINY = 1e-24
CELLS, SLOTS, EXPORT = 64, 256, 32
PIECES = 4
TOGETHER = 8
COUNTS, SLOT_OF, EXPORTS, LOCAL_STARTS, LOCAL_LIST, CROSS_STARTS, CROSS_LIST = 0, 64, 128, 160, 232, 296, 368
LOCAL_FIRST, CROSS_FIRST, PLAN_COUNTS, PLAN_SLOTS, LOCAL_TILES, CROSS_TILES, PLAN_SIZE = 0, 72, 144, 208, 272, 536, 1088
DENSITY_ROWS = 32
FORCE_ROWS = 32
ROOT = math.sqrt(1.5 * SIGMA_NORM)
VMEM, SMEM = pltpu.VMEM, pltpu.SMEM
MESH = pl.DeviceIdType.MESH
DENSITY_PICKED, DENSITY_TURNED = (0, 1, 2, 3), (4,)
FORCE_PICKED = (0, 1, 2, 3, 4, 5, 12)
SIDES = (0, 1, 2, 3, 5, 6, 7, 8)
FORCE_LANES = [(0, 0), (0, 1), (0, 2), (0, 5), (0, 6), (0, 7), (1, 0), (1, 1), (1, 2), (2, 0), (2, 1), (1, 3), (0, 3)]
FORCE_FAR = [(0, 0), (0, 1), (0, 2), (0, 5), (0, 6), (0, 7), (1, 0), (1, 1), (1, 2), (1, 4), (1, 5), (1, 3), (0, 3)]


def over_tiles(plan, start, count, block):
    def tile(index):
        entry = plan[start + index]
        return entry // 2, pl.ds(pl.multiple_of((entry % 2) * 128, 128), 128)

    def two(step, carry):
        block((tile(2 * step), tile(2 * step + 1)))
        return carry

    lax.fori_loop(0, count // 2, two, 0)

    @pl.when(count % 2 == 1)
    def last():
        block((tile(count - 1),))


def over_part(plan, cell, firsts, tiles, block):
    start = plan[firsts + cell]
    over_tiles(plan, tiles + start, plan[firsts + cell + 1] - start, block)


def flipped(row):
    return jnp.transpose(jnp.broadcast_to(row, (128, 128)))


def split(values):
    high = values.astype(jnp.bfloat16)
    rest = values - high.astype(F32)
    middle = rest.astype(jnp.bfloat16)
    return high, middle, (rest - middle.astype(F32)).astype(jnp.bfloat16)


def picker(rows):
    width = 128 * len(rows)
    part = lax.rem(lax.broadcasted_iota(I32, (32, width), 0), 8)
    inside = lax.broadcasted_iota(I32, (32, width), 0) < 24
    block = lax.broadcasted_iota(I32, (32, width), 1) // 128
    wanted = jnp.zeros((32, width), I32)
    for i, row in enumerate(rows):
        wanted = jnp.where(block == i, row, wanted)
    return jnp.where(inside & (part == wanted), 1.0, 0.0).astype(jnp.bfloat16)


def spread(rows, target, cells, counts, size, table8, picked, pick, derive=None):
    def half(place, cell, start):
        made = {}
        parts = split(table8[cell, :, start : start + 128])
        left = jnp.concatenate(parts + (jnp.zeros((8, 128), jnp.bfloat16),), axis=0)
        spreads = lax.dot_general(
            left, pick[...], (((0,), (0,)), ((), ())), preferred_element_type=F32
        )
        for i, slot in enumerate(picked):
            made[slot] = spreads[:, 128 * i : 128 * i + 128]
        for slot, table, row in rows:
            made[slot] = flipped(table[cell, row : row + 1, start : start + 128])
        if derive is not None:
            derive(made)
        for slot, value in made.items():
            target[place * size + slot, start : start + 128, :] = value

    for place, cell in enumerate(cells):
        half(place, cell, 0)
    for place, cell in enumerate(cells):

        @pl.when(counts[place] > 128)
        def second_half():
            half(place, cell, 128)


def over_cells(plan, lay, work):
    def group(step, carry):
        cells = [step * TOGETHER + i for i in range(TOGETHER)]
        lay(cells, [plan[PLAN_COUNTS + cell] for cell in cells])
        lax.fori_loop(0, TOGETHER, lambda i, c: (work(step * TOGETHER + i, i), c)[1], 0)
        return carry

    lax.fori_loop(0, CELLS // TOGETHER, group, 0)


def summed_rows(values):
    return jnp.sum(values.reshape(values.shape[0] // 8, 8, 128), axis=0)


def spline_unscaled(radius, smooth_twice, smooth):
    outer = jnp.maximum(smooth_twice - radius, 0.0)
    inner = jnp.maximum(smooth - radius, 0.0)
    return (0.25 * outer) * (outer * outer) - inner * (inner * inner)


def prepare_kernel(ints, pos, vel, energy, masses, bins, first, second, near, far, note):
    def measure(cell, totals):
        count = ints[COUNTS + cell]
        chunks = (count + (FORCE_ROWS - 1)) // FORCE_ROWS
        tiles = 1 + (count > 128).astype(I32)
        return totals[0] + chunks, totals[1] + tiles, totals[2] + chunks * tiles

    chunks, tiles, both = lax.fori_loop(0, CELLS, measure, (0, 0, 0), unroll=8)
    for k in range(EXPORT):
        note[k] = ints[COUNTS + ints[EXPORTS + k]]
    note[EXPORT] = chunks
    note[EXPORT + 1] = tiles
    note[EXPORT + 2] = both
    for k in range(EXPORT + 3, 128):
        note[k] = 0

    lane = lax.broadcasted_iota(I32, (1, SLOTS), 1)
    smooth = 0.4 * jnp.exp2(bins[...].astype(F32) * math.log2(1.2))
    made = derived_fields(smooth, energy[...])
    for cell in range(CELLS):
        live = (lane < ints[COUNTS + cell]).astype(F32)
        one = slice(cell, cell + 1)
        for axis in range(3):
            first[cell, axis : axis + 1, :] = pos[axis, one, :]
            first[cell, 5 + axis : 6 + axis, :] = vel[axis, one, :]
        first[cell, 3:4, :] = masses[one, :] * live
        first[cell, 4:5, :] = smooth[one, :]
        for i, value in enumerate(made):
            second[cell, i : i + 1, :] = value[one, :]
        second[cell, 4:5, :] = energy[one, :]
        second[cell, 5:6, :] = live

    def gather(k, carry):
        cell = ints[EXPORTS + k]
        near[k] = first[cell]
        far[k] = second[cell, 4:5, :]
        return carry

    lax.fori_loop(0, EXPORT, gather, 0, unroll=8)


def derived_fields(smooth, energy):
    inverse = pl.reciprocal(smooth, approx=True)
    square = inverse * inverse
    sound = jnp.sqrt(GAMMA_GAS * (GAMMA_GAS - 1.0) * energy) * (1.0 / 40.0)
    return (0.5 * ROOT) * (square * inverse), ROOT * square, sound, 0.05 * smooth


def place_of(side):
    rows, columns = lax.axis_size("gx"), lax.axis_size("yz")
    g = lax.rem(lax.axis_index("gx") + (side // 3 - 1 + rows), rows)
    y = lax.rem(lax.axis_index("yz") + (side % 3 - 1 + columns), columns)
    return g, y


def greet(sides):
    barrier = pltpu.get_barrier_semaphore()
    for side in sides:
        pl.semaphore_signal(barrier, inc=1, device_id=place_of(side), device_id_type=MESH)
    pl.semaphore_wait(barrier, len(sides))


def remote(source, target, send, receive, side):
    return pltpu.make_async_remote_copy(
        src_ref=source,
        dst_ref=target,
        send_sem=send,
        recv_sem=receive,
        device_id=place_of(side),
        device_id_type=MESH,
    )


def part_of(ref, side, piece):
    size = EXPORT // PIECES
    return ref.at[pl.ds(side * EXPORT + piece * size, size)]


def greet_lines():
    barrier = pltpu.get_barrier_semaphore()
    rows, columns = lax.axis_size("gx"), lax.axis_size("yz")
    for step in range(1, rows):
        pl.semaphore_signal(barrier, inc=1, device_id=line_place(step, 0), device_id_type=MESH)
    for step in range(1, columns):
        pl.semaphore_signal(barrier, inc=1, device_id=line_place(0, step), device_id_type=MESH)
    pl.semaphore_wait(barrier, rows + columns - 2)


def line_place(down, over):
    rows, columns = lax.axis_size("gx"), lax.axis_size("yz")
    return lax.rem(lax.axis_index("gx") + down, rows), lax.rem(lax.axis_index("yz") + over, columns)


def gather_lines(every, part, steps, send, receive, place):
    copies = []
    for step in range(1, steps):
        copy = pltpu.make_async_remote_copy(
            src_ref=every.at[part],
            dst_ref=every.at[part],
            send_sem=send.at[step],
            recv_sem=receive.at[step],
            device_id=place(step),
            device_id_type=MESH,
        )
        copy.start()
        copies.append(copy)
    return copies


def halo_kernel(
    near, far, note, near_all, far_all, notes, shares, every, send, receive, row_send, row_receive, column_send, column_receive
):
    columns = lax.axis_size("yz")
    line = lax.axis_index("gx") * columns
    notes[4] = note[0]
    every[line + lax.axis_index("yz")] = note[0]
    greet_lines()
    mine = gather_lines(
        every, pl.ds(line + lax.axis_index("yz"), 1), columns, column_send, column_receive,
        lambda step: line_place(0, step),
    )
    kinds = [(near, near_all, p) for p in range(PIECES)] + [(far, far_all, None), (note, notes, None)]
    started = {}

    def view(ref, slot, piece):
        if piece is not None:
            return part_of(ref, slot, piece)
        size = EXPORT if ref is far_all or ref is far else 1
        return ref.at[pl.ds(slot * size, size)]

    for kind, (own, whole, piece) in enumerate(kinds):
        for side in (7, 1, 5, 3):
            slot = 8 - side
            copy = remote(view(own, 0, piece), view(whole, slot, piece), send.at[kind, slot], receive.at[kind, slot], side)
            copy.start()
            started[kind, slot] = copy
    for copy in mine:
        copy.wait()
    lines = gather_lines(
        every, pl.ds(line, columns), lax.axis_size("gx"), row_send, row_receive,
        lambda step: line_place(step, 0),
    )
    for kind, (own, whole, piece) in enumerate(kinds):
        for came in (1, 7):
            started[kind, came].wait_recv()
            for side in (5, 3):
                slot = came + (-1 if side == 5 else 1)
                copy = remote(view(whole, came, piece), view(whole, slot, piece), send.at[kind, slot], receive.at[kind, slot], side)
                copy.start()
                started[kind, slot] = copy
    for copy in lines:
        copy.wait()
    balance(every, shares)
    for (kind, slot), copy in started.items():
        copy.wait_send()
        if slot not in (1, 7):
            copy.wait_recv()


def swap_all(source, target, send, receive, stride):
    copies = []
    for side in SIDES:
        slot = 8 - side
        piece = source.at[pl.ds(side * EXPORT, EXPORT)] if stride else source
        copy = remote(piece, target.at[pl.ds(slot * EXPORT, EXPORT)], send.at[slot], receive.at[slot], side)
        copy.start()
        copies.append(copy)
    for copy in copies:
        copy.wait()


def total_of(block):
    parts = [block[side * EXPORT : (side + 1) * EXPORT] for side in SIDES]
    return ((parts[0] + parts[1]) + (parts[2] + parts[3])) + ((parts[4] + parts[5]) + (parts[6] + parts[7]))


def combine_kernel(ints, first, second, partial, back, raw, late, late_all, came, sent, total, send, receive):
    greet(SIDES)
    swap_all(back, came, send.at[0], receive.at[0], True)
    total[...] = total_of(came)

    def per_cell(cell, carry):
        slot = ints[SLOT_OF + cell]
        extra = jnp.where(slot >= 0, total[jnp.maximum(slot, 0)], 0.0)
        inverse = pl.reciprocal(first[cell, 4:5, :], approx=True)
        cube = inverse * inverse * inverse
        value = (partial[cell] + extra) * (SIGMA_NORM * cube * cube)
        raw[cell] = value
        rho = jnp.where(second[cell, 5:6, :] > 0, value, 1.0)
        late[cell, 0:1, :] = rho * (1.0 / 200.0)
        late[cell, 1:2, :] = (GAMMA_GAS - 1.0) * second[cell, 4:5, :] * pl.reciprocal(rho, approx=True)
        return carry

    lax.fori_loop(0, CELLS, per_cell, 0, unroll=8)

    def gather(k, carry):
        sent[k] = late[ints[EXPORTS + k], 0:1, :]
        return carry

    lax.fori_loop(0, EXPORT, gather, 0, unroll=8)
    swap_all(sent, late_all, send.at[1], receive.at[1], False)


def return_kernel(back, extra, came, send, receive):
    greet(SIDES)
    swap_all(back, came, send, receive, True)
    extra[...] = total_of(came)


def balance(every, shares):
    loads = jnp.transpose(every[:, 0, :].astype(F32))
    chunks, tiles, both = (loads[EXPORT + i : EXPORT + i + 1] for i in range(3))
    local = 0.25 * tiles + 0.04 * both + (0.04 / CELLS) * (chunks * tiles)
    lane = lax.broadcasted_iota(I32, (1, 128), 1)
    columns = lax.axis_size("yz")
    place = lax.rem(lane, columns)

    def over(value, step):
        if step == 0:
            return value
        inner = pltpu.roll(value, (128 - step) % 128, 1)
        wrapped = pltpu.roll(value, (step * (columns - 1)) % 128, 1)
        return jnp.where(place == (columns - 1 if step > 0 else 0), wrapped, inner)

    def along(value, up, step):
        moved_up = pltpu.roll(value, (128 - up * columns) % 128, 1) if up else value
        return over(moved_up, step)

    links = [(side // 3 - 1, side % 3 - 1) for side in (5, 6, 7, 8)]
    scale = 0.043 * EXPORT / (CELLS * CELLS)
    costs = [
        (0.5 * scale) * (chunks * along(tiles, *link) + along(chunks, *link) * tiles) for link in links
    ]
    inverse = [0.1 / jnp.maximum(cost, 1e-3) for cost in costs]

    def step(i, parts):
        total = local
        for link, cost, part in zip(links, costs, parts):
            total = total + part * cost + along((1.0 - part) * cost, -link[0], -link[1])
        return tuple(
            jnp.clip(part + (along(total, *link) - total) * inv, 0.0, 1.0)
            for link, inv, part in zip(links, inverse, parts)
        )

    parts = lax.fori_loop(0, 8, step, (jnp.full((1, 128), 0.5, F32),) * 4)
    me = lax.axis_index("gx") * columns + lax.axis_index("yz")
    for i, (link, part) in enumerate(zip(links, parts)):
        count = jnp.floor(part * EXPORT + 0.5)
        for row, value in ((i, count), (4 + i, along(count, -link[0], -link[1]))):
            mine = jnp.sum(jnp.where(lane == me, value, 0.0), axis=1, keepdims=True)
            shares[row : row + 1, :] = jnp.broadcast_to(mine, (1, 128)).astype(I32)


def make_plan(ints, notes, shares, codes, plan):
    def code(j, carry):
        entry = ints[CROSS_LIST + j]
        source, slot = entry & 1023, ints[SLOT_OF + (entry >> 10)]
        side, place = source >> 5, source & 31
        share = shares[jnp.where(side > 4, side - 5, 7 - side), 0]
        use = jnp.where(side > 4, (place < share).astype(I32), (slot >= share).astype(I32))
        codes[j] = source * 4 + use * (1 + (notes[side, 0, place] > 128).astype(I32))
        return carry

    lax.fori_loop(0, 256, code, 0, unroll=8)

    def put(at, cell):
        plan[at] = 2 * cell
        plan[at + 1] = 2 * cell + 1

    def per_cell(cell, carry):
        local, cross = carry
        plan[LOCAL_FIRST + cell] = local
        plan[CROSS_FIRST + cell] = cross
        count = ints[COUNTS + cell]
        plan[PLAN_COUNTS + cell] = count
        plan[PLAN_SLOTS + cell] = ints[SLOT_OF + cell]
        put(LOCAL_TILES + local, cell)
        local = local + 1 + (count > 128).astype(I32)

        def add_local(j, at):
            target = ints[LOCAL_LIST + j]
            put(LOCAL_TILES + at, target)
            return at + 1 + (ints[COUNTS + target] > 128).astype(I32)

        def add_cross(j, at):
            entry = codes[j]
            put(CROSS_TILES + at, entry >> 2)
            return at + (entry & 3)

        local = lax.fori_loop(ints[LOCAL_STARTS + cell], ints[LOCAL_STARTS + cell + 1], add_local, local)
        cross = lax.fori_loop(ints[CROSS_STARTS + cell], ints[CROSS_STARTS + cell + 1], add_cross, cross)
        return local, cross

    local, cross = lax.fori_loop(0, CELLS, per_cell, (0, 0))
    plan[LOCAL_FIRST + CELLS] = local
    plan[CROSS_FIRST + CELLS] = cross


def density_lanes(held, base, count, table, lanes, add_lane, lane_mass, row_sums):
    size = DENSITY_ROWS
    trips = (count + (size - 1)) // size
    fields = []
    for cell, l in lanes:
        x, y, z, m, h = (table[cell, i : i + 1, l] for i in range(5))
        fields.append((x, y, z, m, h, h + h))

    def chunk(step, totals):
        rows = pl.ds(pl.multiple_of(step * size, size), size)
        rx, ry, rz, mass = (held[base + i, rows, :] for i in range(4))
        if lane_mass:
            rh = held[base + 4, rows, :]
            rh2 = rh + rh
            row_total = row_sums[rows, :]
        result = []
        for total, (x, y, z, m, h1, h2) in zip(totals, fields):
            dx, dy, dz = x - rx, y - ry, z - rz
            dist_sq = jnp.maximum(dx * dx + dy * dy + dz * dz, TINY)
            radius = dist_sq * lax.rsqrt(dist_sq)
            result.append(total + summed_rows(spline_unscaled(radius, h2, h1) * mass))
            if lane_mass:
                row_total = row_total + spline_unscaled(radius, rh2, rh) * m
        if lane_mass:
            row_sums[rows, :] = row_total
        return tuple(result)

    totals = lax.fori_loop(0, trips, chunk, (jnp.zeros((8, 128), F32),) * len(lanes))
    for (cell, l), total in zip(lanes, totals):
        add_lane[cell, :, l] += jnp.sum(total, axis=0, keepdims=True)


def density_kernel(
    ints, notes, shares, table, imports, raw, back, plan, held, sums, codes, pick,
):
    raw[...] = jnp.zeros_like(raw)
    back[...] = jnp.zeros_like(back)
    make_plan(ints, notes, shares, codes, plan)
    pick[...] = picker(DENSITY_PICKED)

    def lay(cells, sizes):
        spread([(i, table, i) for i in DENSITY_TURNED], held, cells, sizes, 5, table, DENSITY_PICKED, pick)

    def work(cell, place):
        base = place * 5
        count = plan[PLAN_COUNTS + cell]
        slot = plan[PLAN_SLOTS + cell]
        over_part(
            plan, cell, LOCAL_FIRST, LOCAL_TILES,
            lambda lanes: density_lanes(held, base, count, table, lanes, raw, False, None),
        )

        @pl.when(slot >= 0)
        def with_pairs():
            sums[...] = jnp.zeros_like(sums)
            over_part(
                plan, cell, CROSS_FIRST, CROSS_TILES,
                lambda lanes: density_lanes(held, base, count, imports, lanes, back, True, sums),
            )

            def finish(l):
                turned = jnp.transpose(sums[l : l + 128, :])
                raw[cell, :, l : l + 128] += jnp.sum(turned, axis=0, keepdims=True)

            finish(0)

            @pl.when(count > 128)
            def second_half():
                finish(128)

    over_cells(plan, lay, work)


def slope_part(radius, half_beta, beta_h):
    reach = half_beta * radius
    outer = jnp.maximum(beta_h - reach, 0.0)
    least = jnp.minimum(outer, reach)
    return least * (outer + (outer - least))


def force_pair(row, lane):
    dx, dy, dz = lane[0] - row[0], lane[1] - row[1], lane[2] - row[2]
    dist_sq = jnp.maximum(dx * dx + dy * dy + dz * dz, TINY)
    inverse = lax.rsqrt(dist_sq)
    radius = dist_sq * inverse
    slope = (slope_part(radius, row[6], row[7]) + slope_part(radius, lane[6], lane[7])) * inverse
    approach = (lane[3] - row[3]) * dx + (lane[4] - row[4]) * dy + (lane[5] - row[5]) * dz
    smooth = lane[11] + row[11]
    converge = (
        smooth * jnp.minimum(approach, 0.0) * pl.reciprocal(dist_sq + smooth * smooth, approx=True)
    )
    viscous = converge * (converge - (lane[8] + row[8])) * pl.reciprocal(lane[9] + row[9], approx=True)
    lane_term = lane[10] + viscous
    row_term = row[10] + viscous
    return dx, dy, dz, slope, approach, lane_term, row_term


def spread_force(tables, held, cells, counts, pick):
    rows = [(i, tables[t], r) for i, (t, r) in enumerate(FORCE_LANES) if i not in (6, 7, 10, 11) + FORCE_PICKED]
    rows.append((13, tables[0], 4))

    def derive(made):
        smooth = made.pop(13)
        inverse = pl.reciprocal(smooth, approx=True)
        square = inverse * inverse
        made[7] = ROOT * square
        made[6] = (0.5 * ROOT) * (square * inverse)
        made[11] = 0.05 * smooth
        made[10] = 4.8 * (made[8] * made[8]) * pl.reciprocal(made[9], approx=True)

    spread(rows, held, cells, counts, 13, tables[0], FORCE_PICKED, pick, derive)


def force_lanes(held, base, count, tables, lanes, add_lane, row_sums, places):
    size = FORCE_ROWS
    trips = (count + (size - 1)) // size
    fields = [[tables[t][cell, i : i + 1, l] for t, i in places] for cell, l in lanes]

    def chunk(step, totals):
        rows = pl.ds(pl.multiple_of(step * size, size), size)
        row = [held[base + i, rows, :] for i in range(13)]
        result = []
        if row_sums is not None:
            row_total = [row_sums[i, rows, :] for i in range(4)]
        for index, lane in enumerate(fields):
            dx, dy, dz, slope, approach, lane_term, row_term = force_pair(row, lane)
            common = lane_term + row_term
            weight = row[12] * slope
            pull = weight * common
            terms = (pull * dx, pull * dy, pull * dz, weight * approach * lane_term)
            result += [t + summed_rows(v) for t, v in zip(totals[4 * index :], terms)]
            if row_sums is not None:
                weight = lane[12] * slope
                pull = weight * common
                terms = (pull * dx, pull * dy, pull * dz, weight * approach * row_term)
                row_total = [t + v for t, v in zip(row_total, terms)]
        if row_sums is not None:
            for i in range(4):
                row_sums[i, rows, :] = row_total[i]
        return tuple(result)

    totals = lax.fori_loop(0, trips, chunk, (jnp.zeros((8, 128), F32),) * (4 * len(lanes)))
    for index, (cell, l) in enumerate(lanes):
        for i in range(4):
            part = jnp.sum(totals[4 * index + i], axis=0, keepdims=True)
            add_lane[cell, i : i + 1, l] += part


def force_kernel(
    plan, first, second, late, imports, energies, densities, own, back, derived, held, row_sums, pick,
):
    own[...] = jnp.zeros_like(own)
    back[...] = jnp.zeros_like(back)
    for side in SIDES:

        def derive(step, carry):
            cells = pl.ds(side * EXPORT + step * 8, 8)
            energy = energies[cells, 0, :]
            rho = densities[cells, 0, :]
            made = derived_fields(imports[cells, 4, :], energy)
            press = (GAMMA_GAS - 1.0) / 200.0 * energy * pl.reciprocal(rho, approx=True)
            for i, value in enumerate(made + (rho, press)):
                derived[cells, i, :] = value
            return carry

        lax.fori_loop(0, EXPORT // 8, derive, 0)
    pick[...] = picker([FORCE_LANES[i][1] for i in FORCE_PICKED])
    tables = (first, second, late)
    far_tables = (imports, derived)

    def lay(cells, sizes):
        spread_force(tables, held, cells, sizes, pick)

    def work(cell, place):
        base = place * 13
        count = plan[PLAN_COUNTS + cell]
        slot = plan[PLAN_SLOTS + cell]
        over_part(
            plan, cell, LOCAL_FIRST, LOCAL_TILES,
            lambda lanes: force_lanes(held, base, count, tables, lanes, own, None, FORCE_LANES),
        )

        @pl.when(slot >= 0)
        def with_pairs():
            row_sums[...] = jnp.zeros_like(row_sums)
            over_part(
                plan, cell, CROSS_FIRST, CROSS_TILES,
                lambda lanes: force_lanes(held, base, count, far_tables, lanes, back, row_sums, FORCE_FAR),
            )

            def finish(l):
                for i in range(4):
                    turned = jnp.transpose(row_sums[i, l : l + 128, :])
                    total = jnp.sum(turned, axis=0, keepdims=True)
                    own[cell, i : i + 1, l : l + 128] += total if i == 3 else -total

            finish(0)

            @pl.when(count > 128)
            def second_half():
                finish(128)

    over_cells(plan, lay, work)


def finish_kernel(ints, second, raw, own, extra, density, acceleration, rate, total):
    total[...] = own[...]

    def add(k, carry):
        total[ints[EXPORTS + k]] += extra[k]
        return carry

    lax.fori_loop(0, EXPORT, add, 0, unroll=4)
    for cell in range(CELLS):
        one = slice(cell, cell + 1)
        live = second[cell, 5:6, :]
        density[one, :] = raw[cell] * live
        for axis in range(3):
            acceleration[axis, one, :] = total[cell, axis : axis + 1, :] * live
        rate[one, :] = -total[cell, 3:4, :] * live


def shape(*dims):
    return jax.ShapeDtypeStruct(dims, F32)


def call(kernel, out, scalars, arrays, scratch, limit=40, collective=None):
    many = isinstance(out, (list, tuple))
    count = len(out) if many else 1
    kinds = [o.dtype for o in out] if many else [out.dtype]
    specs = [
        pl.BlockSpec(memory_space=SMEM if k == I32 and collective is None else VMEM) for k in kinds
    ]
    extra = {} if collective is None else dict(collective_id=collective, has_side_effects=True)
    return pl.pallas_call(
        kernel,
        out_shape=out,
        in_specs=[pl.BlockSpec(memory_space=SMEM)] * len(scalars)
        + [pl.BlockSpec(memory_space=VMEM)] * len(arrays),
        out_specs=specs if many else specs[0],
        scratch_shapes=scratch,
        compiler_params=pltpu.CompilerParams(vmem_limit_bytes=limit << 20, **extra),
    )(*scalars, *arrays)


def grouped(keys, values):
    index = jnp.arange(keys.shape[0], dtype=I32)
    ahead = (keys[None, :] < keys[:, None]) | (
        (keys[None, :] == keys[:, None]) & (index[None, :] < index[:, None])
    )
    place = jnp.sum(ahead.astype(I32), axis=1)
    ordered = jnp.sum(jnp.where(place[None, :] == index[:, None], values[None, :], 0), axis=1)
    cells = jnp.arange(CELLS + 1, dtype=I32)
    starts = jnp.sum((keys[None, :] < cells[:, None]).astype(I32), axis=1)
    return starts, ordered


def body(pos, vel, energy, masses, bins, counts, exports, cross_pairs, local_pairs):
    cell_ids = jnp.arange(CELLS, dtype=I32)
    slots = jnp.arange(EXPORT, dtype=I32)
    is_export = exports[None, :] == cell_ids[:, None]
    slot_of = jnp.sum(jnp.where(is_export, slots[None, :] + 1, 0), axis=1) - 1
    local_starts, local_list = grouped(local_pairs[1], local_pairs[0])
    cross_starts, cross_list = grouped(cross_pairs[0], cross_pairs[1] + 1024 * cross_pairs[0])
    pad = jnp.zeros((7,), I32)
    ints = jnp.concatenate(
        [counts, slot_of, exports, local_starts, pad, local_list, cross_starts, pad, cross_list]
    )
    sems = pltpu.SemaphoreType.DMA
    first, second, near, far, note = call(
        prepare_kernel,
        [shape(CELLS, 8, SLOTS), shape(CELLS, 8, SLOTS), shape(EXPORT, 8, SLOTS), shape(EXPORT, 1, SLOTS),
         jax.ShapeDtypeStruct((128,), I32)],
        [ints],
        [pos, vel, energy, masses, bins],
        [],
        60,
    )
    imports, energies, notes, shares = call(
        halo_kernel,
        [
            shape(9 * EXPORT, 8, SLOTS),
            shape(9 * EXPORT, 1, SLOTS),
            jax.ShapeDtypeStruct((9, 1, 128), I32),
            jax.ShapeDtypeStruct((8, 128), I32),
        ],
        [],
        [near, far, note[None, None]],
        [VMEM((128, 1, 128), I32)] + [sems(d) for d in ((PIECES + 2, 9),) * 2 + ((16,),) * 2 + ((8,),) * 2],
        40,
        0,
    )
    partial, back, plan = call(
        density_kernel,
        [shape(CELLS, 1, SLOTS), shape(9 * EXPORT, 1, SLOTS), jax.ShapeDtypeStruct((PLAN_SIZE,), I32)],
        [ints, notes, shares],
        [first, imports],
        [VMEM((5 * TOGETHER, SLOTS, 128), F32), VMEM((SLOTS, 128), F32), SMEM((256,), I32),
         VMEM((32, 128 * len(DENSITY_PICKED)), jnp.bfloat16)],
    )
    raw, late, densities = call(
        combine_kernel,
        [shape(CELLS, 1, SLOTS), shape(CELLS, 2, SLOTS), shape(9 * EXPORT, 1, SLOTS)],
        [ints],
        [first, second, partial, back],
        [
            VMEM((9 * EXPORT, 1, SLOTS), F32),
            VMEM((EXPORT, 1, SLOTS), F32),
            VMEM((EXPORT, 1, SLOTS), F32),
            sems((2, 9)),
            sems((2, 9)),
        ],
        40,
        1,
    )
    own, back = call(
        force_kernel,
        [shape(CELLS, 4, SLOTS), shape(9 * EXPORT, 4, SLOTS)],
        [plan],
        [first, second, late, imports, energies, densities],
        [
            VMEM((9 * EXPORT, 8, SLOTS), F32),
            VMEM((13 * TOGETHER, SLOTS, 128), F32),
            VMEM((4, SLOTS, 128), F32),
            VMEM((32, 128 * len(FORCE_PICKED)), jnp.bfloat16),
        ],
    )
    came = call(
        return_kernel,
        shape(EXPORT, 4, SLOTS),
        [],
        [back],
        [VMEM((9 * EXPORT, 4, SLOTS), F32), sems((9,)), sems((9,))],
        40,
        2,
    )
    return tuple(
        call(
            finish_kernel,
            [shape(CELLS, SLOTS), shape(3, CELLS, SLOTS), shape(CELLS, SLOTS)],
            [ints],
            [second, raw, own, came],
            [VMEM((CELLS, 4, SLOTS), F32)],
        )
    )


def solution(mesh):
    both = ("gx", "yz")
    return jax.shard_map(
        body,
        mesh=mesh,
        in_specs=(
            P(None, both, None),
            P(None, both, None),
            P(both, None),
            P(both, None),
            P(both, None),
            P(both),
            P(both),
            P(None, both),
            P(None, both),
        ),
        out_specs=(P(both, None), P(None, both, None), P(both, None)),
        check_vma=False,
    )
```

```python
import math

import jax
import jax.numpy as jnp
from jax import lax
from jax.experimental import pallas as pl
from jax.experimental.pallas import tpu as pltpu
from jax.sharding import PartitionSpec as P

F32, I32 = jnp.float32, jnp.int32
SIGMA_NORM = 0.3183098861837907
GAMMA_GAS = 5.0 / 3.0
TINY = 1e-24
CELLS, SLOTS, EXPORT = 64, 256, 32
PIECES = 4
TOGETHER = 8
COUNTS, SLOT_OF, EXPORTS, LOCAL_STARTS, LOCAL_LIST, CROSS_STARTS, CROSS_LIST = 0, 64, 128, 160, 232, 296, 368
LOCAL_FIRST, CROSS_FIRST, PLAN_COUNTS, PLAN_SLOTS, LOCAL_TILES, CROSS_TILES, PLAN_SIZE = 0, 72, 144, 208, 272, 536, 1088
DENSITY_ROWS = 32
FORCE_ROWS = 32
ROOT = math.sqrt(1.5 * SIGMA_NORM)
VMEM, SMEM = pltpu.VMEM, pltpu.SMEM
MESH = pl.DeviceIdType.MESH
DENSITY_PICKED, DENSITY_TURNED = (0, 1, 2, 3), (4,)
FORCE_PICKED = (0, 1, 2, 3, 4, 5, 12)
SIDES = (0, 1, 2, 3, 5, 6, 7, 8)
FORCE_LANES = [(0, 0), (0, 1), (0, 2), (0, 5), (0, 6), (0, 7), (1, 0), (1, 1), (1, 2), (2, 0), (2, 1), (1, 3), (0, 3)]
FORCE_FAR = [(0, 0), (0, 1), (0, 2), (0, 5), (0, 6), (0, 7), (1, 0), (1, 1), (1, 2), (1, 4), (1, 5), (1, 3), (0, 3)]


def over_tiles(plan, start, count, block, fours):
    def tile(index):
        entry = plan[start + index]
        return entry // 2, pl.ds(pl.multiple_of((entry % 2) * 128, 128), 128)

    def two(step, carry):
        block((tile(2 * step), tile(2 * step + 1)))
        return carry

    def four(step, carry):
        block(tuple(tile(4 * step + i) for i in range(4)))
        return carry

    done = 0
    if fours:
        done = count // 4
        lax.fori_loop(0, done, four, 0)
    lax.fori_loop(2 * done, count // 2, two, 0)

    @pl.when(count % 2 == 1)
    def last():
        block((tile(count - 1),))


def over_part(plan, cell, firsts, tiles, block, fours=False):
    start = plan[firsts + cell]
    over_tiles(plan, tiles + start, plan[firsts + cell + 1] - start, block, fours)


def flipped(row):
    return jnp.transpose(jnp.broadcast_to(row, (128, 128)))


def split(values):
    high = values.astype(jnp.bfloat16)
    rest = values - high.astype(F32)
    middle = rest.astype(jnp.bfloat16)
    return high, middle, (rest - middle.astype(F32)).astype(jnp.bfloat16)


def picker(rows):
    width = 128 * len(rows)
    part = lax.rem(lax.broadcasted_iota(I32, (32, width), 0), 8)
    inside = lax.broadcasted_iota(I32, (32, width), 0) < 24
    block = lax.broadcasted_iota(I32, (32, width), 1) // 128
    wanted = jnp.zeros((32, width), I32)
    for i, row in enumerate(rows):
        wanted = jnp.where(block == i, row, wanted)
    return jnp.where(inside & (part == wanted), 1.0, 0.0).astype(jnp.bfloat16)


def spread(rows, target, cells, counts, size, table8, picked, pick, derive=None):
    def half(place, cell, start):
        made = {}
        parts = split(table8[cell, :, start : start + 128])
        left = jnp.concatenate(parts + (jnp.zeros((8, 128), jnp.bfloat16),), axis=0)
        spreads = lax.dot_general(
            left, pick[...], (((0,), (0,)), ((), ())), preferred_element_type=F32
        )
        for i, slot in enumerate(picked):
            made[slot] = spreads[:, 128 * i : 128 * i + 128]
        for slot, table, row in rows:
            made[slot] = flipped(table[cell, row : row + 1, start : start + 128])
        if derive is not None:
            derive(made)
        for slot, value in made.items():
            target[place * size + slot, start : start + 128, :] = value

    for place, cell in enumerate(cells):
        half(place, cell, 0)
    for place, cell in enumerate(cells):

        @pl.when(counts[place] > 128)
        def second_half():
            half(place, cell, 128)


def over_cells(plan, lay, work):
    def group(step, carry):
        cells = [step * TOGETHER + i for i in range(TOGETHER)]
        lay(cells, [plan[PLAN_COUNTS + cell] for cell in cells])
        lax.fori_loop(0, TOGETHER, lambda i, c: (work(step * TOGETHER + i, i), c)[1], 0)
        return carry

    lax.fori_loop(0, CELLS // TOGETHER, group, 0)


def summed_rows(values):
    return jnp.sum(values.reshape(values.shape[0] // 8, 8, 128), axis=0)


def spline_unscaled(radius, smooth_twice, smooth):
    outer = jnp.maximum(smooth_twice - radius, 0.0)
    inner = jnp.maximum(smooth - radius, 0.0)
    return (0.25 * outer) * (outer * outer) - inner * (inner * inner)


def prepare_kernel(ints, pos, vel, energy, masses, bins, first, second, near, far, note):
    def measure(cell, totals):
        count = ints[COUNTS + cell]
        chunks = (count + (FORCE_ROWS - 1)) // FORCE_ROWS
        tiles = 1 + (count > 128).astype(I32)
        return totals[0] + chunks, totals[1] + tiles, totals[2] + chunks * tiles

    chunks, tiles, both = lax.fori_loop(0, CELLS, measure, (0, 0, 0), unroll=8)
    for k in range(EXPORT):
        note[k] = ints[COUNTS + ints[EXPORTS + k]]
    note[EXPORT] = chunks
    note[EXPORT + 1] = tiles
    note[EXPORT + 2] = both
    for k in range(EXPORT + 3, 128):
        note[k] = 0

    lane = lax.broadcasted_iota(I32, (1, SLOTS), 1)
    smooth = 0.4 * jnp.exp2(bins[...].astype(F32) * math.log2(1.2))
    made = derived_fields(smooth, energy[...])
    for cell in range(CELLS):
        live = (lane < ints[COUNTS + cell]).astype(F32)
        one = slice(cell, cell + 1)
        for axis in range(3):
            first[cell, axis : axis + 1, :] = pos[axis, one, :]
            first[cell, 5 + axis : 6 + axis, :] = vel[axis, one, :]
        first[cell, 3:4, :] = masses[one, :] * live
        first[cell, 4:5, :] = smooth[one, :]
        for i, value in enumerate(made):
            second[cell, i : i + 1, :] = value[one, :]
        second[cell, 4:5, :] = energy[one, :]
        second[cell, 5:6, :] = live

    def gather(k, carry):
        cell = ints[EXPORTS + k]
        near[k] = first[cell]
        far[k] = second[cell, 4:5, :]
        return carry

    lax.fori_loop(0, EXPORT, gather, 0, unroll=8)


def derived_fields(smooth, energy):
    inverse = pl.reciprocal(smooth, approx=True)
    square = inverse * inverse
    sound = jnp.sqrt(GAMMA_GAS * (GAMMA_GAS - 1.0) * energy) * (1.0 / 40.0)
    return (0.5 * ROOT) * (square * inverse), ROOT * square, sound, 0.05 * smooth


def place_of(side):
    rows, columns = lax.axis_size("gx"), lax.axis_size("yz")
    g = lax.rem(lax.axis_index("gx") + (side // 3 - 1 + rows), rows)
    y = lax.rem(lax.axis_index("yz") + (side % 3 - 1 + columns), columns)
    return g, y


def greet(sides):
    barrier = pltpu.get_barrier_semaphore()
    for side in sides:
        pl.semaphore_signal(barrier, inc=1, device_id=place_of(side), device_id_type=MESH)
    pl.semaphore_wait(barrier, len(sides))


def remote(source, target, send, receive, side):
    return pltpu.make_async_remote_copy(
        src_ref=source,
        dst_ref=target,
        send_sem=send,
        recv_sem=receive,
        device_id=place_of(side),
        device_id_type=MESH,
    )


def part_of(ref, side, piece):
    size = EXPORT // PIECES
    return ref.at[pl.ds(side * EXPORT + piece * size, size)]


def greet_lines():
    barrier = pltpu.get_barrier_semaphore()
    rows, columns = lax.axis_size("gx"), lax.axis_size("yz")
    for step in range(1, rows):
        pl.semaphore_signal(barrier, inc=1, device_id=line_place(step, 0), device_id_type=MESH)
    for step in range(1, columns):
        pl.semaphore_signal(barrier, inc=1, device_id=line_place(0, step), device_id_type=MESH)
    pl.semaphore_wait(barrier, rows + columns - 2)


def line_place(down, over):
    rows, columns = lax.axis_size("gx"), lax.axis_size("yz")
    return lax.rem(lax.axis_index("gx") + down, rows), lax.rem(lax.axis_index("yz") + over, columns)


def gather_lines(every, part, steps, send, receive, place):
    copies = []
    for step in range(1, steps):
        copy = pltpu.make_async_remote_copy(
            src_ref=every.at[part],
            dst_ref=every.at[part],
            send_sem=send.at[step],
            recv_sem=receive.at[step],
            device_id=place(step),
            device_id_type=MESH,
        )
        copy.start()
        copies.append(copy)
    return copies


def halo_kernel(
    near, far, note, near_all, far_all, notes, shares, every, send, receive, row_send, row_receive, column_send, column_receive
):
    columns = lax.axis_size("yz")
    line = lax.axis_index("gx") * columns
    notes[4] = note[0]
    every[line + lax.axis_index("yz")] = note[0]
    greet_lines()
    mine = gather_lines(
        every, pl.ds(line + lax.axis_index("yz"), 1), columns, column_send, column_receive,
        lambda step: line_place(0, step),
    )
    kinds = [(near, near_all, p) for p in range(PIECES)] + [(far, far_all, None), (note, notes, None)]
    started = {}

    def view(ref, slot, piece):
        if piece is not None:
            return part_of(ref, slot, piece)
        size = EXPORT if ref is far_all or ref is far else 1
        return ref.at[pl.ds(slot * size, size)]

    for kind, (own, whole, piece) in enumerate(kinds):
        for side in (7, 1, 5, 3):
            slot = 8 - side
            copy = remote(view(own, 0, piece), view(whole, slot, piece), send.at[kind, slot], receive.at[kind, slot], side)
            copy.start()
            started[kind, slot] = copy
    for copy in mine:
        copy.wait()
    lines = gather_lines(
        every, pl.ds(line, columns), lax.axis_size("gx"), row_send, row_receive,
        lambda step: line_place(step, 0),
    )
    for kind, (own, whole, piece) in enumerate(kinds):
        for came in (1, 7):
            started[kind, came].wait_recv()
            for side in (5, 3):
                slot = came + (-1 if side == 5 else 1)
                copy = remote(view(whole, came, piece), view(whole, slot, piece), send.at[kind, slot], receive.at[kind, slot], side)
                copy.start()
                started[kind, slot] = copy
    for copy in lines:
        copy.wait()
    balance(every, shares)
    for (kind, slot), copy in started.items():
        copy.wait_send()
        if slot not in (1, 7):
            copy.wait_recv()


def swap_all(source, target, send, receive, stride):
    copies = []
    for side in SIDES:
        slot = 8 - side
        piece = source.at[pl.ds(side * EXPORT, EXPORT)] if stride else source
        copy = remote(piece, target.at[pl.ds(slot * EXPORT, EXPORT)], send.at[slot], receive.at[slot], side)
        copy.start()
        copies.append(copy)
    for copy in copies:
        copy.wait()


def total_of(block):
    parts = [block[side * EXPORT : (side + 1) * EXPORT] for side in SIDES]
    return ((parts[0] + parts[1]) + (parts[2] + parts[3])) + ((parts[4] + parts[5]) + (parts[6] + parts[7]))


def combine_kernel(ints, first, second, partial, back, raw, late, late_all, came, sent, total, send, receive):
    greet(SIDES)
    swap_all(back, came, send.at[0], receive.at[0], True)
    total[...] = total_of(came)

    def per_cell(cell, carry):
        slot = ints[SLOT_OF + cell]
        extra = jnp.where(slot >= 0, total[jnp.maximum(slot, 0)], 0.0)
        inverse = pl.reciprocal(first[cell, 4:5, :], approx=True)
        cube = inverse * inverse * inverse
        value = (partial[cell] + extra) * (SIGMA_NORM * cube * cube)
        raw[cell] = value
        rho = jnp.where(second[cell, 5:6, :] > 0, value, 1.0)
        late[cell, 0:1, :] = rho * (1.0 / 200.0)
        late[cell, 1:2, :] = (GAMMA_GAS - 1.0) * second[cell, 4:5, :] * pl.reciprocal(rho, approx=True)
        return carry

    lax.fori_loop(0, CELLS, per_cell, 0, unroll=8)

    def gather(k, carry):
        sent[k] = late[ints[EXPORTS + k], 0:1, :]
        return carry

    lax.fori_loop(0, EXPORT, gather, 0, unroll=8)
    swap_all(sent, late_all, send.at[1], receive.at[1], False)


def return_kernel(back, extra, came, send, receive):
    greet(SIDES)
    swap_all(back, came, send, receive, True)
    extra[...] = total_of(came)


def balance(every, shares):
    loads = jnp.transpose(every[:, 0, :].astype(F32))
    chunks, tiles, both = (loads[EXPORT + i : EXPORT + i + 1] for i in range(3))
    local = 0.25 * tiles + 0.04 * both + (0.04 / CELLS) * (chunks * tiles)
    lane = lax.broadcasted_iota(I32, (1, 128), 1)
    columns = lax.axis_size("yz")
    place = lax.rem(lane, columns)

    def over(value, step):
        if step == 0:
            return value
        inner = pltpu.roll(value, (128 - step) % 128, 1)
        wrapped = pltpu.roll(value, (step * (columns - 1)) % 128, 1)
        return jnp.where(place == (columns - 1 if step > 0 else 0), wrapped, inner)

    def along(value, up, step):
        moved_up = pltpu.roll(value, (128 - up * columns) % 128, 1) if up else value
        return over(moved_up, step)

    links = [(side // 3 - 1, side % 3 - 1) for side in (5, 6, 7, 8)]
    scale = 0.043 * EXPORT / (CELLS * CELLS)
    costs = [
        (0.5 * scale) * (chunks * along(tiles, *link) + along(chunks, *link) * tiles) for link in links
    ]
    inverse = [0.1 / jnp.maximum(cost, 1e-3) for cost in costs]

    def step(i, parts):
        total = local
        for link, cost, part in zip(links, costs, parts):
            total = total + part * cost + along((1.0 - part) * cost, -link[0], -link[1])
        return tuple(
            jnp.clip(part + (along(total, *link) - total) * inv, 0.0, 1.0)
            for link, inv, part in zip(links, inverse, parts)
        )

    parts = lax.fori_loop(0, 8, step, (jnp.full((1, 128), 0.5, F32),) * 4)
    me = lax.axis_index("gx") * columns + lax.axis_index("yz")
    for i, (link, part) in enumerate(zip(links, parts)):
        count = jnp.floor(part * EXPORT + 0.5)
        for row, value in ((i, count), (4 + i, along(count, -link[0], -link[1]))):
            mine = jnp.sum(jnp.where(lane == me, value, 0.0), axis=1, keepdims=True)
            shares[row : row + 1, :] = jnp.broadcast_to(mine, (1, 128)).astype(I32)


def make_plan(ints, notes, shares, codes, plan):
    def code(j, carry):
        entry = ints[CROSS_LIST + j]
        source, slot = entry & 1023, ints[SLOT_OF + (entry >> 10)]
        side, place = source >> 5, source & 31
        share = shares[jnp.where(side > 4, side - 5, 7 - side), 0]
        use = jnp.where(side > 4, (place < share).astype(I32), (slot >= share).astype(I32))
        codes[j] = source * 4 + use * (1 + (notes[side, 0, place] > 128).astype(I32))
        return carry

    lax.fori_loop(0, 256, code, 0, unroll=8)

    def put(at, cell):
        plan[at] = 2 * cell
        plan[at + 1] = 2 * cell + 1

    def per_cell(cell, carry):
        local, cross = carry
        plan[LOCAL_FIRST + cell] = local
        plan[CROSS_FIRST + cell] = cross
        count = ints[COUNTS + cell]
        plan[PLAN_COUNTS + cell] = count
        plan[PLAN_SLOTS + cell] = ints[SLOT_OF + cell]
        put(LOCAL_TILES + local, cell)
        local = local + 1 + (count > 128).astype(I32)

        def add_local(j, at):
            target = ints[LOCAL_LIST + j]
            put(LOCAL_TILES + at, target)
            return at + 1 + (ints[COUNTS + target] > 128).astype(I32)

        def add_cross(j, at):
            entry = codes[j]
            put(CROSS_TILES + at, entry >> 2)
            return at + (entry & 3)

        local = lax.fori_loop(ints[LOCAL_STARTS + cell], ints[LOCAL_STARTS + cell + 1], add_local, local)
        cross = lax.fori_loop(ints[CROSS_STARTS + cell], ints[CROSS_STARTS + cell + 1], add_cross, cross)
        return local, cross

    local, cross = lax.fori_loop(0, CELLS, per_cell, (0, 0))
    plan[LOCAL_FIRST + CELLS] = local
    plan[CROSS_FIRST + CELLS] = cross


def density_lanes(held, base, count, table, lanes, add_lane, lane_mass, row_sums):
    size = DENSITY_ROWS
    trips = (count + (size - 1)) // size
    fields = []
    for cell, l in lanes:
        x, y, z, m, h = (table[cell, i : i + 1, l] for i in range(5))
        fields.append((x, y, z, m, h, h + h))

    def chunk(step, totals):
        rows = pl.ds(pl.multiple_of(step * size, size), size)
        rx, ry, rz, mass = (held[base + i, rows, :] for i in range(4))
        if lane_mass:
            rh = held[base + 4, rows, :]
            rh2 = rh + rh
            row_total = row_sums[rows, :]
        result = []
        for total, (x, y, z, m, h1, h2) in zip(totals, fields):
            dx, dy, dz = x - rx, y - ry, z - rz
            dist_sq = jnp.maximum(dx * dx + dy * dy + dz * dz, TINY)
            radius = dist_sq * lax.rsqrt(dist_sq)
            result.append(total + summed_rows(spline_unscaled(radius, h2, h1) * mass))
            if lane_mass:
                row_total = row_total + spline_unscaled(radius, rh2, rh) * m
        if lane_mass:
            row_sums[rows, :] = row_total
        return tuple(result)

    totals = lax.fori_loop(0, trips, chunk, (jnp.zeros((8, 128), F32),) * len(lanes))
    for (cell, l), total in zip(lanes, totals):
        add_lane[cell, :, l] += jnp.sum(total, axis=0, keepdims=True)


def density_kernel(
    ints, notes, shares, table, imports, raw, back, plan, held, sums, codes, pick,
):
    raw[...] = jnp.zeros_like(raw)
    back[...] = jnp.zeros_like(back)
    make_plan(ints, notes, shares, codes, plan)
    pick[...] = picker(DENSITY_PICKED)

    def lay(cells, sizes):
        spread([(i, table, i) for i in DENSITY_TURNED], held, cells, sizes, 5, table, DENSITY_PICKED, pick)

    def work(cell, place):
        base = place * 5
        count = plan[PLAN_COUNTS + cell]
        slot = plan[PLAN_SLOTS + cell]
        over_part(
            plan, cell, LOCAL_FIRST, LOCAL_TILES,
            lambda lanes: density_lanes(held, base, count, table, lanes, raw, False, None),
            True,
        )

        @pl.when(slot >= 0)
        def with_pairs():
            sums[...] = jnp.zeros_like(sums)
            over_part(
                plan, cell, CROSS_FIRST, CROSS_TILES,
                lambda lanes: density_lanes(held, base, count, imports, lanes, back, True, sums),
                True,
            )

            def finish(l):
                turned = jnp.transpose(sums[l : l + 128, :])
                raw[cell, :, l : l + 128] += jnp.sum(turned, axis=0, keepdims=True)

            finish(0)

            @pl.when(count > 128)
            def second_half():
                finish(128)

    over_cells(plan, lay, work)


def slope_part(radius, half_beta, beta_h):
    reach = half_beta * radius
    outer = jnp.maximum(beta_h - reach, 0.0)
    least = jnp.minimum(outer, reach)
    return least * (outer + (outer - least))


def force_pair(row, lane):
    dx, dy, dz = lane[0] - row[0], lane[1] - row[1], lane[2] - row[2]
    dist_sq = jnp.maximum(dx * dx + dy * dy + dz * dz, TINY)
    inverse = lax.rsqrt(dist_sq)
    radius = dist_sq * inverse
    slope = (slope_part(radius, row[6], row[7]) + slope_part(radius, lane[6], lane[7])) * inverse
    approach = (lane[3] - row[3]) * dx + (lane[4] - row[4]) * dy + (lane[5] - row[5]) * dz
    smooth = lane[11] + row[11]
    converge = (
        smooth * jnp.minimum(approach, 0.0) * pl.reciprocal(dist_sq + smooth * smooth, approx=True)
    )
    viscous = converge * (converge - (lane[8] + row[8])) * pl.reciprocal(lane[9] + row[9], approx=True)
    lane_term = lane[10] + viscous
    row_term = row[10] + viscous
    return dx, dy, dz, slope, approach, lane_term, row_term


def spread_force(tables, held, cells, counts, pick):
    rows = [(i, tables[t], r) for i, (t, r) in enumerate(FORCE_LANES) if i not in (6, 7, 10, 11) + FORCE_PICKED]
    rows.append((13, tables[0], 4))

    def derive(made):
        smooth = made.pop(13)
        inverse = pl.reciprocal(smooth, approx=True)
        square = inverse * inverse
        made[7] = ROOT * square
        made[6] = (0.5 * ROOT) * (square * inverse)
        made[11] = 0.05 * smooth
        made[10] = 4.8 * (made[8] * made[8]) * pl.reciprocal(made[9], approx=True)

    spread(rows, held, cells, counts, 13, tables[0], FORCE_PICKED, pick, derive)


def force_lanes(held, base, count, tables, lanes, add_lane, row_sums, places):
    size = FORCE_ROWS
    trips = (count + (size - 1)) // size
    fields = [[tables[t][cell, i : i + 1, l] for t, i in places] for cell, l in lanes]

    def chunk(step, totals):
        rows = pl.ds(pl.multiple_of(step * size, size), size)
        row = [held[base + i, rows, :] for i in range(13)]
        result = []
        if row_sums is not None:
            row_total = [row_sums[i, rows, :] for i in range(4)]
        for index, lane in enumerate(fields):
            dx, dy, dz, slope, approach, lane_term, row_term = force_pair(row, lane)
            common = lane_term + row_term
            weight = row[12] * slope
            pull = weight * common
            terms = (pull * dx, pull * dy, pull * dz, weight * approach * lane_term)
            result += [t + summed_rows(v) for t, v in zip(totals[4 * index :], terms)]
            if row_sums is not None:
                weight = lane[12] * slope
                pull = weight * common
                terms = (pull * dx, pull * dy, pull * dz, weight * approach * row_term)
                row_total = [t + v for t, v in zip(row_total, terms)]
        if row_sums is not None:
            for i in range(4):
                row_sums[i, rows, :] = row_total[i]
        return tuple(result)

    totals = lax.fori_loop(0, trips, chunk, (jnp.zeros((8, 128), F32),) * (4 * len(lanes)))
    for index, (cell, l) in enumerate(lanes):
        for i in range(4):
            part = jnp.sum(totals[4 * index + i], axis=0, keepdims=True)
            add_lane[cell, i : i + 1, l] += part


def force_kernel(
    plan, first, second, late, imports, energies, densities, own, back, derived, held, row_sums, pick,
):
    own[...] = jnp.zeros_like(own)
    back[...] = jnp.zeros_like(back)
    for side in SIDES:

        def derive(step, carry):
            cells = pl.ds(side * EXPORT + step * 8, 8)
            energy = energies[cells, 0, :]
            rho = densities[cells, 0, :]
            made = derived_fields(imports[cells, 4, :], energy)
            press = (GAMMA_GAS - 1.0) / 200.0 * energy * pl.reciprocal(rho, approx=True)
            for i, value in enumerate(made + (rho, press)):
                derived[cells, i, :] = value
            return carry

        lax.fori_loop(0, EXPORT // 8, derive, 0)
    pick[...] = picker([FORCE_LANES[i][1] for i in FORCE_PICKED])
    tables = (first, second, late)
    far_tables = (imports, derived)

    def lay(cells, sizes):
        spread_force(tables, held, cells, sizes, pick)

    def work(cell, place):
        base = place * 13
        count = plan[PLAN_COUNTS + cell]
        slot = plan[PLAN_SLOTS + cell]
        over_part(
            plan, cell, LOCAL_FIRST, LOCAL_TILES,
            lambda lanes: force_lanes(held, base, count, tables, lanes, own, None, FORCE_LANES),
        )

        @pl.when(slot >= 0)
        def with_pairs():
            row_sums[...] = jnp.zeros_like(row_sums)
            over_part(
                plan, cell, CROSS_FIRST, CROSS_TILES,
                lambda lanes: force_lanes(held, base, count, far_tables, lanes, back, row_sums, FORCE_FAR),
            )

            def finish(l):
                for i in range(4):
                    turned = jnp.transpose(row_sums[i, l : l + 128, :])
                    total = jnp.sum(turned, axis=0, keepdims=True)
                    own[cell, i : i + 1, l : l + 128] += total if i == 3 else -total

            finish(0)

            @pl.when(count > 128)
            def second_half():
                finish(128)

    over_cells(plan, lay, work)


def finish_kernel(ints, second, raw, own, extra, density, acceleration, rate, total):
    total[...] = own[...]

    def add(k, carry):
        total[ints[EXPORTS + k]] += extra[k]
        return carry

    lax.fori_loop(0, EXPORT, add, 0, unroll=4)
    for cell in range(CELLS):
        one = slice(cell, cell + 1)
        live = second[cell, 5:6, :]
        density[one, :] = raw[cell] * live
        for axis in range(3):
            acceleration[axis, one, :] = total[cell, axis : axis + 1, :] * live
        rate[one, :] = -total[cell, 3:4, :] * live


def shape(*dims):
    return jax.ShapeDtypeStruct(dims, F32)


def call(kernel, out, scalars, arrays, scratch, limit=40, collective=None):
    many = isinstance(out, (list, tuple))
    count = len(out) if many else 1
    kinds = [o.dtype for o in out] if many else [out.dtype]
    specs = [
        pl.BlockSpec(memory_space=SMEM if k == I32 and collective is None else VMEM) for k in kinds
    ]
    extra = {} if collective is None else dict(collective_id=collective, has_side_effects=True)
    return pl.pallas_call(
        kernel,
        out_shape=out,
        in_specs=[pl.BlockSpec(memory_space=SMEM)] * len(scalars)
        + [pl.BlockSpec(memory_space=VMEM)] * len(arrays),
        out_specs=specs if many else specs[0],
        scratch_shapes=scratch,
        compiler_params=pltpu.CompilerParams(vmem_limit_bytes=limit << 20, **extra),
    )(*scalars, *arrays)


def grouped(keys, values):
    index = jnp.arange(keys.shape[0], dtype=I32)
    ahead = (keys[None, :] < keys[:, None]) | (
        (keys[None, :] == keys[:, None]) & (index[None, :] < index[:, None])
    )
    place = jnp.sum(ahead.astype(I32), axis=1)
    ordered = jnp.sum(jnp.where(place[None, :] == index[:, None], values[None, :], 0), axis=1)
    cells = jnp.arange(CELLS + 1, dtype=I32)
    starts = jnp.sum((keys[None, :] < cells[:, None]).astype(I32), axis=1)
    return starts, ordered


def body(pos, vel, energy, masses, bins, counts, exports, cross_pairs, local_pairs):
    cell_ids = jnp.arange(CELLS, dtype=I32)
    slots = jnp.arange(EXPORT, dtype=I32)
    is_export = exports[None, :] == cell_ids[:, None]
    slot_of = jnp.sum(jnp.where(is_export, slots[None, :] + 1, 0), axis=1) - 1
    local_starts, local_list = grouped(local_pairs[1], local_pairs[0])
    cross_starts, cross_list = grouped(cross_pairs[0], cross_pairs[1] + 1024 * cross_pairs[0])
    pad = jnp.zeros((7,), I32)
    ints = jnp.concatenate(
        [counts, slot_of, exports, local_starts, pad, local_list, cross_starts, pad, cross_list]
    )
    sems = pltpu.SemaphoreType.DMA
    first, second, near, far, note = call(
        prepare_kernel,
        [shape(CELLS, 8, SLOTS), shape(CELLS, 8, SLOTS), shape(EXPORT, 8, SLOTS), shape(EXPORT, 1, SLOTS),
         jax.ShapeDtypeStruct((128,), I32)],
        [ints],
        [pos, vel, energy, masses, bins],
        [],
        60,
    )
    imports, energies, notes, shares = call(
        halo_kernel,
        [
            shape(9 * EXPORT, 8, SLOTS),
            shape(9 * EXPORT, 1, SLOTS),
            jax.ShapeDtypeStruct((9, 1, 128), I32),
            jax.ShapeDtypeStruct((8, 128), I32),
        ],
        [],
        [near, far, note[None, None]],
        [VMEM((128, 1, 128), I32)] + [sems(d) for d in ((PIECES + 2, 9),) * 2 + ((16,),) * 2 + ((8,),) * 2],
        40,
        0,
    )
    partial, back, plan = call(
        density_kernel,
        [shape(CELLS, 1, SLOTS), shape(9 * EXPORT, 1, SLOTS), jax.ShapeDtypeStruct((PLAN_SIZE,), I32)],
        [ints, notes, shares],
        [first, imports],
        [VMEM((5 * TOGETHER, SLOTS, 128), F32), VMEM((SLOTS, 128), F32), SMEM((256,), I32),
         VMEM((32, 128 * len(DENSITY_PICKED)), jnp.bfloat16)],
    )
    raw, late, densities = call(
        combine_kernel,
        [shape(CELLS, 1, SLOTS), shape(CELLS, 2, SLOTS), shape(9 * EXPORT, 1, SLOTS)],
        [ints],
        [first, second, partial, back],
        [
            VMEM((9 * EXPORT, 1, SLOTS), F32),
            VMEM((EXPORT, 1, SLOTS), F32),
            VMEM((EXPORT, 1, SLOTS), F32),
            sems((2, 9)),
            sems((2, 9)),
        ],
        40,
        1,
    )
    own, back = call(
        force_kernel,
        [shape(CELLS, 4, SLOTS), shape(9 * EXPORT, 4, SLOTS)],
        [plan],
        [first, second, late, imports, energies, densities],
        [
            VMEM((9 * EXPORT, 8, SLOTS), F32),
            VMEM((13 * TOGETHER, SLOTS, 128), F32),
            VMEM((4, SLOTS, 128), F32),
            VMEM((32, 128 * len(FORCE_PICKED)), jnp.bfloat16),
        ],
    )
    came = call(
        return_kernel,
        shape(EXPORT, 4, SLOTS),
        [],
        [back],
        [VMEM((9 * EXPORT, 4, SLOTS), F32), sems((9,)), sems((9,))],
        40,
        2,
    )
    return tuple(
        call(
            finish_kernel,
            [shape(CELLS, SLOTS), shape(3, CELLS, SLOTS), shape(CELLS, SLOTS)],
            [ints],
            [second, raw, own, came],
            [VMEM((CELLS, 4, SLOTS), F32)],
        )
    )


def solution(mesh):
    both = ("gx", "yz")
    return jax.shard_map(
        body,
        mesh=mesh,
        in_specs=(
            P(None, both, None),
            P(None, both, None),
            P(both, None),
            P(both, None),
            P(both, None),
            P(both),
            P(both),
            P(None, both),
            P(None, both),
        ),
        out_specs=(P(both, None), P(None, both, None), P(both, None)),
        check_vma=False,
    )
```
